256 devices in a mesh: dp: 32 (over x, z_lo, core), expert: 8 (over y, z_hi).
Axes of the slice: x: 4, y: 4, z: 8 (z_hi: 2, z_lo: 4; z = z_hi * 4 + z_lo), core: 2. Of those that a mesh axis runs over, the one named last changes fastest.
Arguments:
- queries: bfloat16 [2, 128, 4096], P(None, 'dp'), may hold values from -170 to 170
- fresh_entries: bfloat16 [2, 128, 512], P(None, 'dp'), may hold values from -6 to 6
- cache_blocks: bfloat16 [128, 32, 128, 512], P('dp', None, 'expert'), may hold values from -6 to 6
- lengths: int32 [128], P('dp'), may hold values from 256 to 4096, as said below
- migration: int32 [256, 2], P('dp'), may hold values from 0 to 31, as said below
- residual: bfloat16 [2, 128, 4096], P(None, 'dp'), may hold values from -6 to 6
- out_weight: bfloat16 [4096, 4096], P('expert'), may hold values from -1.5 to 1.5
- norm_gain: float32 [4096], replicated, may hold values from 0.1 to 1.9
- routes: int32 [2, 128, 8], P(None, 'dp'), may hold values from 0 to 63, all different within a row; in each aligned block of 4 rows (0 to 3, 4 to 7, ..., all dimensions but the last counted through in order) at most 2 rows name the same one
- route_gates: float32 [2, 128, 8], P(None, 'dp'), may hold values from 0.1 to 1
- w_gate: bfloat16 [64, 4096, 1024], P('dp', None, 'expert'), may hold values from -0.09375 to 0.09375
- w_up: bfloat16 [64, 4096, 1024], P('dp', None, 'expert'), may hold values from -0.09375 to 0.09375
- w_down: bfloat16 [64, 1024, 4096], P('dp', 'expert'), may hold values from -0.1875 to 0.1875
Outputs:
- layer_out: bfloat16 [2, 128, 4096], P(None, 'dp', 'expert')
- guest_blocks: bfloat16 [256, 128, 512], P('dp', 'expert')
The draws below stay inside these ranges and needn't reach their ends.
Inputs may be any that keep to these rules, and one draw needn't show every extreme that they name: `lengths`: the longest request of every draw has all 4096 positions. `migration`: rows s * 8 to s * 8 + 7 name distinct pairs of a request of index s of dp (0 to 3) and a block that lies wholly below that request's length; the last block of the longest request is among them. `routes`: each row names 8 different experts; in each step the rows of one index of dp name one expert at most 2 times, a bound that some block reaches in some step and index.
All inputs are finite; a program needn't handle non-finite values.
Results may differ from the reference program's by a relative error of at most 0.027.
Values may be sent and summed in bfloat16 or wider, within the bound.
A program may use at most 320 MiB of HBM per device.

```python
import math
import jax
import jax.numpy as jnp
import numpy as np
from jax import lax

D = 4096
HD = 128
QH = 32
KVH = 2
FF = 1024
TOPK = 8
REQ_DEV = 4
BLOCKS = 32
EXPERTS = 64
MOST = 2
BLK = 128
REQS = 128
MIG = 8
N_DP = 32


def shared_cache(key):
    raw_vals = jax.random.normal(key, (REQS, BLOCKS, BLK, 2 * KVH * HD), jnp.float32)
    return jnp.clip(raw_vals, -6.0, 6.0)


def longest_request(key):
    return jax.random.randint(jax.random.fold_in(key, 23), (), 0, N_DP * REQ_DEV)


def load_plan(key):
    group_load = jax.random.randint(jax.random.fold_in(key, 21), (N_DP, 1), 1, 5)
    spread_len = jax.random.randint(jax.random.fold_in(key, 22), (N_DP, REQ_DEV), 0, BLOCKS * BLK - 2 * BLK + 1)
    flat_len = (2 * BLK + spread_len * group_load // 4).reshape(-1)
    longest = longest_request(key)
    flat_len = jnp.where(jnp.arange(N_DP * REQ_DEV) == longest, BLOCKS * BLK, flat_len)
    return flat_len.astype(jnp.int32)


def draw_cache_blocks(key, part):
    base_vals = shared_cache(key)
    return base_vals.astype(jnp.bfloat16)


def draw_queries(key, part):
    key = jax.random.fold_in(key, 5)
    raw_vals = jnp.clip(jax.random.normal(key, (2, REQS, QH * HD), jnp.float32), -6.0, 6.0)
    return raw_vals.astype(jnp.bfloat16)


def draw_lengths(key, part):
    return load_plan(key)


def draw_migration(key, part):
    plan_len = load_plan(key)
    longest = longest_request(key)
    key = jax.random.fold_in(key, 9)
    full_blocks = plan_len.reshape(N_DP, REQ_DEV) // BLK
    block_ids = jnp.arange(BLOCKS, dtype=jnp.int32)
    usable = (block_ids[None, None, :] < full_blocks[:, :, None]).reshape(N_DP, REQ_DEV * BLOCKS)
    pair_total = REQ_DEV * BLOCKS
    noise_vals = jax.random.randint(key, (N_DP, pair_total), 0, 4096)
    flat_idx = jnp.arange(pair_total, dtype=jnp.int32)
    ranking = jnp.where(usable, noise_vals * pair_total + flat_idx[None, :] + 1, -flat_idx[None, :] - 1)
    forced_group = longest // REQ_DEV
    forced_pair = longest % REQ_DEV * BLOCKS + BLOCKS - 1
    is_forced = (jnp.arange(N_DP, dtype=jnp.int32)[:, None] == forced_group) & (flat_idx[None, :] == forced_pair)
    ranking = jnp.where(is_forced, 4096 * pair_total + pair_total + 1, ranking)
    top_vals, picked = lax.top_k(ranking, MIG)
    request_part = picked // BLOCKS
    block_part = picked % BLOCKS
    return jnp.stack([request_part, block_part], -1).reshape(N_DP * MIG, 2).astype(jnp.int32)


def level_of(stream_key, extent, split, smallest, largest):
    factor_of, own = 1.0, jax.random.fold_in(stream_key, 6)
    for dim, parts in split:
        steps = jnp.exp(jax.random.uniform(jax.random.fold_in(own, dim), (parts,), jnp.float32, smallest / len(split), largest / len(split)))
        factor_of = factor_of * jnp.repeat(steps, extent[dim] // parts).reshape([-1 if axis == dim else 1 for axis in range(len(extent))])
    return factor_of


def shared_out(rng, own, number, rows, number_of, top, most, slope):
    order = jax.random.permutation(rng, number_of)
    heavy_load, usual = shares(number_of, rows * top, most, slope, True), shares(number_of, rows * top, most, slope, False)
    places = jnp.arange(number_of)

    def named(tallies, offset_by):
        used = int((tallies > 0).sum())
        fixed = max(1, used // 4)
        shifted = fixed + (places - fixed + offset_by * (used - fixed)) % max(1, number_of - fixed)
        return jnp.zeros((number_of,), jnp.int32).at[order[jnp.where(places < fixed, places, shifted)]].set(jnp.asarray(tallies, jnp.int32))

    tallies = jnp.where(number % 4 == 0, named(heavy_load, number // 4), named(usual, number - number // 4 - 1))
    mixed = jax.random.permutation(jax.random.fold_in(own, 3), number_of)
    source_of, taker = mixed[0:number_of // 2 * 2:2], mixed[1:number_of // 2 * 2:2]
    margin = jnp.minimum(tallies[source_of] - 1, most - tallies[taker]) // 2
    margin = jnp.where((source_of == order[0]) | (taker == order[0]) | (tallies[taker] == 0), 0, jnp.maximum(margin, 0))
    shifted = jax.random.randint(jax.random.fold_in(own, 4), (number_of // 2,), 0, 1 << 20) % (margin + 1)
    tallies = tallies.at[source_of].add(-shifted).at[taker].add(shifted)
    items = jnp.searchsorted(jnp.cumsum(tallies), jnp.arange(rows * top), side="right").astype(jnp.int32)
    listing = items.reshape(top, rows).T
    listing = listing[jax.random.permutation(jax.random.fold_in(own, 1), rows)]
    offset_by = jax.random.randint(jax.random.fold_in(own, 2), (rows, 1), 0, top)
    return jnp.take_along_axis(listing, (jnp.arange(top)[None, :] + offset_by) % top, axis=1)


def shares(amount, total, reach, skew, full):
    loads = [(1 << 20) // math.isqrt(standing ** skew) + 1 for standing in range(1, amount + 1)]
    largest = reach if full else min(reach, max(-(-total // amount), total * loads[0] // sum(loads)))
    least = 1 if total - largest >= amount - 1 else 0
    holding, rest = [largest] + [least] * (amount - 1), total - largest - least * (amount - 1)
    while rest > 0:
        candidates = [i for i in range(1, amount) if holding[i] < largest] or [i for i in range(1, amount) if holding[i] < reach]
        mass, budget = sum([loads[i] for i in candidates]), rest
        for i in candidates:
            extra = min(reach - holding[i], max(1, budget * loads[i] // mass), rest)
            holding[i] = holding[i] + extra
            rest = rest - extra
    return np.array(holding)


def gaussian(rng, dims, width, bound, cuts=(), kind=jnp.bfloat16):
    array = jax.random.normal(rng, dims, jnp.float32) * width
    if len(cuts) > 0:
        array = level_of(rng, dims, cuts, -0.22, 0.18) * array
    return jnp.clip(array, min=-bound, max=bound).astype(kind)


def setup_inputs(seed: int = 0) -> dict:
    seeds = jax.random.split(jax.random.key(seed), 14)
    queries = draw_queries(jax.random.fold_in(seeds[13], 71), 0)
    fresh_entries = gaussian(seeds[1], (2, REQS, 2 * KVH * HD), 1.0, 6.0, ((1, 32),))
    cache_blocks = draw_cache_blocks(jax.random.fold_in(seeds[13], 71), 0)
    lengths = draw_lengths(jax.random.fold_in(seeds[13], 71), 0)
    migration = draw_migration(jax.random.fold_in(seeds[13], 71), 0)
    residual = gaussian(seeds[5], (2, REQS, D), 1.0, 6.0, ((1, 32),))
    out_weight = gaussian(seeds[6], (QH * HD, D), (HD // 8) ** -0.5, 1.5, ((0, 8),))
    norm_gain = jnp.clip(1.0 + 0.18 * jax.random.normal(seeds[7], (D,), jnp.float32), 0.1, 1.9)
    routes_keys = jax.random.split(jax.random.fold_in(seeds[8], 1), 2 * REQS // REQ_DEV)
    routes_turns = jax.random.permutation(jax.random.fold_in(seeds[8], 3), 2 * REQS // REQ_DEV)
    routes = jax.vmap(lambda own, number: shared_out(jax.random.fold_in(seeds[8], 2), own, number, REQ_DEV, EXPERTS, TOPK, MOST, 1))(routes_keys, routes_turns).reshape((2, REQS, TOPK))
    route_gates = jnp.clip(jnp.exp(math.log(1.0) - 2.3025851 * jax.random.uniform(seeds[9], (2, REQS, TOPK), jnp.float32) ** level_of(seeds[9], (2, REQS, TOPK), ((1, 32),), -0.2, 0.2)), 0.1, 1.0)
    w_gate = gaussian(seeds[10], (EXPERTS, D, FF), D ** -0.5, 0.09375, ((0, 32), (2, 8)))
    w_up = gaussian(seeds[11], (EXPERTS, D, FF), D ** -0.5, 0.09375, ((0, 32), (2, 8)))
    w_down = gaussian(seeds[12], (EXPERTS, FF, D), FF ** -0.5, 0.1875, ((0, 32), (1, 8)))
    return {"queries": queries, "fresh_entries": fresh_entries, "cache_blocks": cache_blocks, "lengths": lengths, "migration": migration, "residual": residual, "out_weight": out_weight, "norm_gain": norm_gain, "routes": routes, "route_gates": route_gates, "w_gate": w_gate, "w_up": w_up, "w_down": w_down}


HIGHEST = lax.Precision.HIGHEST

def attend_request(inputs):
    cache_row, length, query_row, fresh_row = inputs
    groups = QH // KVH
    score_scale = 1.0 / HD ** 0.5
    stored = cache_row.reshape(BLOCKS * BLK, 2, KVH, HD).astype(jnp.float32)
    fresh_kv = fresh_row.reshape(2, 2, KVH, HD).astype(jnp.float32)
    is_valid = jnp.arange(BLOCKS * BLK, dtype=jnp.int32) < length
    results = []
    for step_idx in range(2):
        query_now = query_row[step_idx].reshape(KVH, groups, HD).astype(jnp.float32)
        keys_all = jnp.concatenate([stored[:, 0], fresh_kv[:step_idx + 1, 0]], 0)
        values_all = jnp.concatenate([stored[:, 1], fresh_kv[:step_idx + 1, 1]], 0)
        usable = jnp.concatenate([is_valid, jnp.ones((step_idx + 1,), jnp.bool_)])
        scores = jnp.einsum('kgd,pkd->kgp', query_now, keys_all, precision=HIGHEST) * score_scale
        scores = jnp.where(usable, scores, -jnp.inf)
        row_peak = lax.optimization_barrier(jnp.max(scores, -1, keepdims=True))
        weights = jnp.exp(scores - row_peak)
        row_total = lax.optimization_barrier(jnp.sum(weights, -1))
        rounded = lax.optimization_barrier(weights.astype(jnp.bfloat16)).astype(jnp.float32)
        summed = jnp.einsum('kgp,pkd->kgd', rounded, values_all, precision=HIGHEST)
        results.append((summed / row_total[..., None]).astype(jnp.bfloat16).reshape(QH * HD))
    return jnp.stack(results)

def expert_mix(tokens_in, route_ids, gate_vals, w_gate, w_up, w_down):
    flat_ids = route_ids.reshape(-1)
    flat_gate = gate_vals.reshape(-1)
    pair_total = REQS * TOPK
    cap_all = N_DP * MOST
    pair_order = jnp.arange(pair_total, dtype=jnp.int32)
    owner_tok = pair_order // TOPK

    def one_expert(running, expert_id):
        ranking = jnp.where(flat_ids == expert_id, 2 * pair_total - pair_order, -pair_order)
        top_vals, picked = lax.top_k(ranking, cap_all)
        chosen = flat_ids[picked] == expert_id
        row_block = tokens_in[owner_tok[picked]]
        gate_part = jnp.dot(row_block, w_gate[expert_id], preferred_element_type=jnp.float32)
        up_part = jnp.dot(row_block, w_up[expert_id], preferred_element_type=jnp.float32)
        inner_act = (jax.nn.silu(gate_part) * up_part).astype(jnp.bfloat16)
        produced = jnp.dot(inner_act, w_down[expert_id], preferred_element_type=jnp.float32)
        produced = lax.optimization_barrier(produced.astype(jnp.bfloat16)).astype(jnp.float32)
        factor = jnp.where(chosen, flat_gate[picked], jnp.zeros_like(flat_gate[picked]))
        return (running.at[owner_tok[picked]].add(factor[:, None] * produced), None)
    start_sum = jnp.zeros((REQS, D), jnp.float32)
    mixed_part, unused = lax.scan(one_expert, start_sum, jnp.arange(EXPERTS, dtype=jnp.int32))
    return mixed_part

def reference(queries, fresh_entries, cache_blocks, lengths, migration, residual, out_weight, norm_gain, routes, route_gates, w_gate, w_up, w_down):
    attended = lax.map(attend_request, (cache_blocks, lengths, jnp.swapaxes(queries, 0, 1), jnp.swapaxes(fresh_entries, 0, 1)))
    outputs = []
    for step_idx in range(2):
        attention = attended[:, step_idx]
        projected = jnp.dot(attention, out_weight, preferred_element_type=jnp.float32)
        hidden = residual[step_idx].astype(jnp.float32) + projected
        spread = lax.optimization_barrier(jnp.mean(hidden * hidden, -1, keepdims=True))
        normed = (hidden * lax.rsqrt(spread + 1e-06) * norm_gain).astype(jnp.bfloat16)
        mixed_part = expert_mix(normed, routes[step_idx], route_gates[step_idx], w_gate, w_up, w_down)
        outputs.append((hidden + mixed_part).astype(jnp.bfloat16))
    layer_out = jnp.stack(outputs)
    source = (jnp.arange(N_DP, dtype=jnp.int32) - N_DP // 2) % N_DP
    rows_idx = (source[:, None] * MIG + jnp.arange(MIG, dtype=jnp.int32)[None, :]).reshape(-1)
    chosen_moves = migration[rows_idx]
    request_idx = rows_idx // MIG * REQ_DEV + chosen_moves[:, 0]
    guest_blocks = cache_blocks[request_idx, chosen_moves[:, 1]]
    return (layer_out, guest_blocks)
```

```python
import math

import jax
import jax.numpy as jnp
from jax import lax
from jax.sharding import PartitionSpec as P

HD = 128
QH = 32
KVH = 2
TOPK = 8
BLOCKS = 32
EXPERTS = 64


def shards(
    queries,
    fresh_entries,
    cache_blocks,
    lengths,
    migration,
    residual,
    out_weight,
    norm_gain,
    routes,
    route_gates,
    w_gate,
    w_up,
    w_down,
):
    n_p = lax.axis_size("expert")
    n_dp = lax.axis_size("dp")
    pos = lax.axis_index("expert")
    me = lax.axis_index("dp")
    reqs = cache_blocks.shape[0]
    rows = cache_blocks.shape[2]
    groups = QH // KVH
    own = QH // n_p
    width = out_weight.shape[1]
    part = width // n_p
    tokens = 2 * reqs
    scale = 1.0 / math.sqrt(HD)

    picked = cache_blocks[migration[:, 0], migration[:, 1]]
    half = n_dp // 2
    guest = lax.ppermute(picked, "dp", [(s, (s + half) % n_dp) for s in range(n_dp)])

    expert_ids = jnp.arange(EXPERTS, dtype=jnp.int32)
    coef = jnp.sum(
        jnp.where(routes[..., None] == expert_ids, route_gates[..., None], 0.0), 2
    ).reshape(tokens, EXPERTS)
    coef_all = lax.all_gather(coef, "dp").reshape(n_dp * tokens, EXPERTS)

    positions = (
        jnp.arange(BLOCKS, dtype=jnp.int32)[:, None] * (rows * n_p)
        + pos * rows
        + jnp.arange(rows, dtype=jnp.int32)[None, :]
    ).reshape(-1)
    valid = positions[None, :] < lengths[:, None]
    stored = cache_blocks.reshape(reqs, BLOCKS * rows, 2, KVH, HD)
    q = queries.reshape(2, reqs, KVH, groups, HD)
    scores = (
        jnp.einsum("srkgd,rpkd->rksgp", q, stored[:, :, 0], preferred_element_type=jnp.float32)
        * scale
    )
    scores = jnp.where(valid[:, None, None, None, :], scores, -jnp.inf)
    peak = jnp.max(scores, -1)
    weights = jnp.exp(scores - peak[..., None])
    total = jnp.sum(weights, -1)
    weighted = jnp.einsum(
        "rksgp,rpkd->rksgd",
        weights.astype(jnp.bfloat16),
        stored[:, :, 1],
        preferred_element_type=jnp.float32,
    )

    def to_owner(v):
        v = jnp.moveaxis(v, 2, 0).reshape((2, reqs, n_p, own) + v.shape[4:])
        return jnp.moveaxis(v, 2, 0)

    state = to_owner(weighted).astype(jnp.bfloat16)
    stats = jnp.stack([to_owner(peak), to_owner(total)], -1)
    state = lax.all_to_all(state, "expert", 0, 0, tiled=True).astype(jnp.float32)
    stats = lax.all_to_all(stats, "expert", 0, 0, tiled=True)
    peaks, totals = stats[..., 0], stats[..., 1]

    kv = pos * own // groups
    fresh = fresh_entries.reshape(2, reqs, 2, KVH, HD).astype(jnp.float32)
    fresh = lax.dynamic_index_in_dim(fresh, kv, 3, keepdims=False)
    q_own = lax.dynamic_slice_in_dim(
        queries.reshape(2, reqs, QH, HD), pos * own, own, 2
    ).astype(jnp.float32)
    f_scores = jnp.sum(q_own[:, None] * fresh[None, :, :, 0][:, :, :, None], -1) * scale
    seen = jnp.arange(2)[None, :] <= jnp.arange(2)[:, None]
    f_scores = jnp.where(seen[:, :, None, None], f_scores, -jnp.inf)
    top = jnp.maximum(jnp.max(peaks, 0), jnp.max(f_scores, 1))
    w_dev = jnp.exp(peaks - top)
    f_w = jnp.exp(f_scores - top[:, None])
    denom = jnp.sum(w_dev * totals, 0) + jnp.sum(f_w, 1)
    numer = jnp.sum(w_dev[..., None] * state, 0) + jnp.sum(
        f_w[..., None] * fresh[None, :, :, 1][:, :, :, None], 1
    )
    attention = (numer / denom[..., None]).astype(jnp.bfloat16).reshape(tokens, own * HD)
    projected = jnp.dot(attention, out_weight, preferred_element_type=jnp.float32)
    projected = lax.psum_scatter(
        projected.astype(jnp.bfloat16), "expert", scatter_dimension=1, tiled=True
    ).astype(jnp.float32)
    res = lax.dynamic_slice_in_dim(residual.reshape(tokens, width), pos * part, part, 1)
    hidden = res.astype(jnp.float32) + projected

    gathered = lax.all_gather(hidden.astype(jnp.bfloat16), ("dp", "expert"))
    gathered = jnp.moveaxis(gathered.reshape(n_dp, n_p, tokens, part), 1, 2)
    gathered = gathered.reshape(n_dp * tokens, width).astype(jnp.float32)
    spread = jnp.mean(gathered * gathered, -1, keepdims=True)
    normed = (gathered * lax.rsqrt(spread + 1e-06) * norm_gain).astype(jnp.bfloat16)
    gate = jnp.einsum("td,jdf->tjf", normed, w_gate, preferred_element_type=jnp.float32)
    up = jnp.einsum("td,jdf->tjf", normed, w_up, preferred_element_type=jnp.float32)
    n_e = w_gate.shape[0]
    coef_own = lax.dynamic_slice_in_dim(coef_all, me * n_e, n_e, 1)
    act = (jax.nn.silu(gate) * up * coef_own[..., None]).astype(jnp.bfloat16)
    mixed = jnp.dot(
        act.reshape(n_dp * tokens, -1),
        w_down.reshape(-1, width),
        preferred_element_type=jnp.float32,
    ).astype(jnp.bfloat16)
    mixed = jnp.moveaxis(mixed.reshape(n_dp, tokens, n_p, part), 2, 1)
    mixed = mixed.reshape(n_dp * n_p, tokens, part)
    mixed = lax.psum_scatter(mixed, ("dp", "expert"), scatter_dimension=0)
    out = (hidden + mixed.astype(jnp.float32)).astype(jnp.bfloat16)
    return (out.reshape(2, reqs, part), guest)


def solution(mesh):
    in_specs = (
        P(None, "dp", None),
        P(None, "dp", None),
        P("dp", None, "expert", None),
        P("dp"),
        P("dp", None),
        P(None, "dp", None),
        P("expert", None),
        P(),
        P(None, "dp", None),
        P(None, "dp", None),
        P("dp", None, "expert"),
        P("dp", None, "expert"),
        P("dp", "expert", None),
    )
    out_specs = (P(None, "dp", "expert"), P("dp", "expert", None))
    return jax.shard_map(shards, mesh=mesh, in_specs=in_specs, out_specs=out_specs, check_vma=False)
```

```python
import functools
import math

import jax
import jax.numpy as jnp
from jax import lax
from jax.experimental import pallas as pl
from jax.experimental.pallas import tpu as pltpu
from jax.sharding import PartitionSpec as P

MESH = pl.DeviceIdType.MESH
HD = 128
QH = 32
KVH = 2
TOPK = 8
BLOCKS = 32
NX, NZL, NY, NZH = 4, 4, 4, 2
N_P = NY * NZH
N_Z = NZH * NZL
N_DP = NX * NZL * 2
REQS = 4
TOK = 2 * REQS
D = 4096
PART = D // N_P
HALF = PART // 2
ROWS = 16
POSN = BLOCKS * ROWS
OWN = QH // N_P
ALL = N_DP * TOK
F32 = jnp.float32
BF16 = jnp.bfloat16
NEG = -1e30
N_SEMS = 72
MIB = 1024 * 1024


def kernel(
    q_ref,
    fresh_ref,
    cache_ref,
    len_ref,
    mig_ref,
    res_ref,
    ow_ref,
    gain_ref,
    routes_ref,
    gates_ref,
    wg_ref,
    wu_ref,
    wd_ref,
    out_ref,
    guest_ref,
    cache_v,
    ow_v,
    wgu_v,
    wd_v,
    picked_v,
    q_s,
    q_b,
    f_s,
    r_s,
    a_send,
    a_recv,
    b_send,
    b_recv,
    hid,
    rt,
    g_buf,
    acc,
    ssq,
    act,
    p_buf,
    s_buf,
    m_buf,
    a_in,
    a_mid,
    n_buf,
    b_in,
    b_mid,
    n2_buf,
    z_send,
    z_recv,
    o_s,
    load_sem,
    send_sem,
    recv_sem,
):
    me = lax.axis_index("dp")
    p = lax.axis_index("expert")
    core = lax.rem(me, 2)
    zlo = lax.rem(lax.div(me, 2), NZL)
    x = lax.div(me, 2 * NZL)
    y = lax.div(p, NZH)
    zhi = lax.rem(p, NZH)
    z = zhi * NZL + zlo

    def place(x_, y_, zlo_, zhi_, core_):
        return ((x_ * NZL + zlo_) * 2 + core_, y_ * NZH + zhi_)

    def at_p(k):
        return (me, lax.rem(p + k, N_P))

    def at_z(k):
        t = lax.rem(z + k, N_Z)
        return place(x, y, lax.rem(t, NZL), lax.div(t, NZL), core)

    def at_x(k):
        return place(lax.rem(x + k, NX), y, zlo, zhi, core)

    def at_zlo(k):
        return place(x, y, lax.rem(zlo + k, NZL), zhi, core)

    def at_a(k):
        return place(lax.rem(x + (1 - core) * k, NX), lax.rem(y + core * k, NY), zlo, zhi, core)

    def at_b(k):
        return place(lax.rem(x + core * k, NX), lax.rem(y + (1 - core) * k, NY), zlo, zhi, core)

    sibling = place(x, y, zlo, zhi, 1 - core)
    ia = (1 - core) * x + core * y
    ib = core * x + (1 - core) * y
    sib_ia = core * x + (1 - core) * y

    loads = []

    def load(src, dst):
        cp = pltpu.make_async_copy(src, dst, load_sem.at[len(loads)])
        cp.start()
        loads.append(cp)
        return cp

    cache_cp = [load(cache_ref.at[r], cache_v.at[r]) for r in range(REQS)]
    ow_cp = load(ow_ref, ow_v)
    w_cp = []
    for j in range(2):
        w_cp.append(load(wg_ref.at[j], wgu_v.at[:, pl.ds(256 * j, 128)]))
        w_cp.append(load(wu_ref.at[j], wgu_v.at[:, pl.ds(256 * j + 128, 128)]))
    wd_cp = [load(wd_ref.at[j], wd_v.at[pl.ds(128 * j, 128)]) for j in range(2)]

    barrier = pltpu.get_barrier_semaphore()
    peers = [at_p(k) for k in range(1, N_P)]
    peers += [at_z(k) for k in range(1, N_Z) if k != NZL]
    peers += [at_x(k) for k in range(1, NX)]
    peers += [sibling]
    for peer in peers:
        pl.semaphore_signal(barrier, inc=1, device_id=peer, device_id_type=MESH)

    sent = []

    def send(src, dst, peer):
        k = len(sent)
        cp = pltpu.make_async_remote_copy(
            src_ref=src,
            dst_ref=dst,
            send_sem=send_sem.at[k],
            recv_sem=recv_sem.at[k],
            device_id=peer,
            device_id_type=MESH,
        )
        cp.start()
        sent.append(cp)
        return cp

    lane = lax.broadcasted_iota(jnp.int32, (REQS, 128), 1)
    for s in range(2):
        ids = routes_ref[s]
        vals = gates_ref[s]
        coef = jnp.zeros((REQS, 128), F32)
        for k in range(TOPK):
            coef = coef + jnp.where(lane == ids[:, k : k + 1], vals[:, k : k + 1], 0.0)
        rt[core, x, zlo, pl.ds(REQS * s, REQS), :] = coef

    for s in range(2):
        q_s[pl.ds(REQS * s, REQS), :] = q_ref[s].astype(F32)
        r_s[pl.ds(REQS * s, REQS), :] = res_ref[
            s, :, pl.ds(pl.multiple_of(p * PART, PART), PART)
        ].astype(F32)
    q_b[...] = jnp.concatenate(
        [q_s[:, h * HD : (h + 1) * HD] for h in range(QH)], axis=0
    ).astype(BF16)

    for cp in cache_cp:
        cp.wait()
    for m in range(8):
        picked_v[m] = cache_v[mig_ref[m, 0], mig_ref[m, 1]]

    scale = 1.0 / math.sqrt(HD)
    col = lax.broadcasted_iota(jnp.int32, (TOK, POSN), 1)
    row = lax.rem(lax.broadcasted_iota(jnp.int32, (TOK, POSN), 0), REQS)
    position = lax.div(col, ROWS) * (ROWS * N_P) + p * ROWS + lax.rem(col, ROWS)
    limit = jnp.full((TOK, POSN), 0, jnp.int32)
    for r in range(REQS):
        limit = jnp.where(row == r, len_ref[r], limit)
    valid = position < limit
    hk = QH // KVH * TOK
    rid = lax.rem(lax.broadcasted_iota(jnp.int32, (hk, POSN), 0), REQS)
    rid_o = lax.rem(lax.broadcasted_iota(jnp.int32, (hk, HD), 0), REQS)
    sub = lax.broadcasted_iota(jnp.int32, (OWN * TOK, 128), 0)
    lan = lax.broadcasted_iota(jnp.int32, (OWN * TOK, 128), 1)
    for k in range(KVH):
        qk = q_b[k * hk : (k + 1) * hk]
        scores = None
        for r in range(REQS):
            keys = cache_v[r, :, :, k * HD : (k + 1) * HD].reshape(POSN, HD)
            part = lax.dot_general(
                qk, keys, (((1,), (1,)), ((), ())), preferred_element_type=F32
            )
            scores = part if r == 0 else jnp.where(rid == r, part, scores)
        scores = scores.reshape(hk // TOK, TOK, POSN)
        scores = jnp.where(valid[None], scores * scale, NEG)
        peak = jnp.max(scores, -1, keepdims=True).astype(BF16).astype(F32)
        weights = jnp.exp(scores - peak)
        total = jnp.sum(weights, -1, keepdims=True)
        weights = weights.reshape(hk, POSN).astype(BF16)
        state = None
        for r in range(REQS):
            vals = cache_v[r, :, :, (KVH + k) * HD : (KVH + k + 1) * HD].reshape(POSN, HD)
            part = jnp.dot(weights, vals, preferred_element_type=F32)
            state = part if r == 0 else jnp.where(rid_o == r, part, state)
        peak = peak.reshape(hk, 1)
        total = total.reshape(hk, 1)
        total_hi = total.astype(BF16).astype(F32)
        total_lo = total - total_hi
        n_rows = OWN * TOK
        for i in range(hk // n_rows):
            dest = k * (hk // n_rows) + i
            rows = slice(i * n_rows, (i + 1) * n_rows)
            a_send[dest, 0:n_rows, :] = state[rows].astype(BF16)
            stat = jnp.where(lan == sub, peak[rows], 0.0)
            stat = jnp.where(lan == sub + n_rows, total_hi[rows], stat)
            stat = jnp.where(lan == sub + 2 * n_rows, total_lo[rows], stat)
            stat = jnp.sum(stat, axis=0, keepdims=True)
            a_send[dest, n_rows : n_rows + 16, :] = jnp.broadcast_to(stat, (16, 128)).astype(BF16)

    pl.semaphore_wait(barrier, len(peers))

    a_cp = []
    for k in range(1, N_P):
        a_cp.append(send(a_send.at[lax.rem(p + k, N_P)], a_recv.at[k], at_p(k)))
    rt_cp = [
        send(rt.at[core, x, zlo], rt.at[core, x, zlo], at_zlo(k)) for k in range(1, NZL)
    ]
    guest_cp = send(picked_v, guest_ref, at_x(2))
    a_recv[0] = a_send[p]

    kv = lax.div(p, N_P // KVH)
    for n in range(2):
        for j in range(2):
            new = fresh_ref[
                n, :, pl.ds(pl.multiple_of((j * KVH + kv) * HD, HD), HD)
            ].astype(F32)
            f_s[n, j, 0:REQS, :] = new
            f_s[n, j, REQS:TOK, :] = new
    q_own = q_s[:, pl.ds(pl.multiple_of(p * PART, PART), PART)]
    q_own = jnp.stack([q_own[:, i * HD : (i + 1) * HD] for i in range(OWN)], axis=0)
    f_scores = [
        jnp.sum(q_own * f_s[n, 0][None], -1, keepdims=True) * scale for n in range(2)
    ]
    step_row = lax.broadcasted_iota(jnp.int32, (OWN, TOK, 1), 1)
    f_scores[1] = jnp.where(step_row >= REQS, f_scores[1], NEG)

    for cp in a_cp:
        cp.wait_recv()
    n_rows = OWN * TOK
    peaks, totals = [], []
    for k in range(N_P):
        stat = a_recv[k, n_rows : n_rows + 16, :].astype(F32)[0:1]
        peaks.append(jnp.sum(jnp.where(lan == sub, stat, 0.0), -1, keepdims=True))
        in_total = (lan == sub + n_rows) | (lan == sub + 2 * n_rows)
        totals.append(jnp.sum(jnp.where(in_total, stat, 0.0), -1, keepdims=True))
    f_scores = [f.reshape(n_rows, 1) for f in f_scores]
    top = jnp.maximum(f_scores[0], f_scores[1])
    for k in range(N_P):
        top = jnp.maximum(top, peaks[k])
    denom = jnp.zeros((n_rows, 1), F32)
    numer = jnp.zeros((n_rows, HD), F32)
    for n in range(2):
        w = jnp.exp(f_scores[n] - top)
        denom = denom + w
        vals = jnp.broadcast_to(f_s[n, 1][None], (OWN, TOK, HD)).reshape(n_rows, HD)
        numer = numer + w * vals
    for k in range(N_P):
        w = jnp.exp(peaks[k] - top)
        denom = denom + w * totals[k]
        numer = numer + w * a_recv[k, 0:n_rows, :].astype(F32)
    attention = (numer / denom).reshape(OWN, TOK, HD)
    attention = jnp.concatenate([attention[i] for i in range(OWN)], axis=1).astype(BF16)

    for cp in rt_cp:
        cp.wait_recv()
    rt_cp = [send(rt.at[core, x], rt.at[core, x], at_x(k)) for k in range(1, NX)]

    def packed(v):
        return jnp.concatenate([v[:, 0:HALF], v[:, HALF:PART]], axis=0)

    def unpacked(v):
        return jnp.concatenate([v[0:TOK], v[TOK : 2 * TOK]], axis=1)

    ow_cp.wait()
    b_cp = []
    for k in range(1, N_P + 1):
        pp = lax.rem(p + k, N_P)
        term = jnp.dot(
            attention,
            ow_v[:, pl.ds(pl.multiple_of(pp * PART, PART), PART)],
            preferred_element_type=F32,
        )
        if k < N_P:
            b_send[k] = packed(term).astype(BF16)
            b_cp.append(send(b_send.at[k], b_recv.at[k], at_p(k)))
    for cp in rt_cp:
        cp.wait_recv()
    rt_cp = [send(rt.at[core], rt.at[core], sibling)]
    hidden = packed(r_s[...] + term)
    for k in range(1, N_P):
        b_cp[k - 1].wait_recv()
        hidden = hidden + b_recv[k].astype(F32)
    hid[...] = hidden
    g_buf[core, ia, ib, z] = hidden.astype(BF16)

    mine = g_buf.at[core, ia, ib, z]
    z_cp = [send(mine, mine, at_z(k)) for k in range(1, N_Z)]
    for cp in z_cp:
        cp.wait_recv()

    def ring_gather(ref, i, n, at):
        lo, hi = pl.ds(0, n // 2), pl.ds(n // 2, n // 2)
        left = lax.rem(i + 3, 4)
        right = lax.rem(i + 1, 4)
        r_lo = send(ref.at[i, lo], ref.at[i, lo], at(1))
        l_hi = send(ref.at[i, hi], ref.at[i, hi], at(3))
        r_hi = send(ref.at[i, hi], ref.at[i, hi], at(1))
        l_lo = send(ref.at[i, lo], ref.at[i, lo], at(3))
        r_lo.wait_recv()
        f_lo = send(ref.at[left, lo], ref.at[left, lo], at(1))
        l_hi.wait_recv()
        f_hi = send(ref.at[right, hi], ref.at[right, hi], at(3))
        return (r_hi, l_lo, f_lo, f_hi)

    def ring_wait(cps):
        for cp in cps:
            cp.wait_recv()

    ring_wait(ring_gather(g_buf.at[core, ia], ib, N_Z, at_b))
    plane = g_buf.at[core]
    rest = ring_gather(plane, ia, 4, at_a)

    def across(j):
        return send(plane.at[j], plane.at[j], sibling)

    c_cp = [across(ia)]
    rest[0].wait_recv()
    c_cp.append(across(lax.rem(ia + 3, 4)))
    rest[1].wait_recv()
    c_cp.append(across(lax.rem(ia + 1, 4)))
    ring_wait(rest[2:])
    c_cp.append(across(lax.rem(ia + 2, 4)))
    ring_wait(c_cp)
    ring_wait(rt_cp)

    for cp in w_cp:
        cp.wait()
    acc[...] = jnp.zeros_like(acc)
    ssq[...] = jnp.zeros_like(ssq)

    def up_step(i, _):
        yy, zz = lax.div(i, NZH), lax.rem(i, NZH)
        zs = pl.ds(pl.multiple_of(zz * NZL, NZL), NZL)
        halves = []
        for blocks in (g_buf[0, :, yy, zs], g_buf[1, yy, :, zs]):
            blocks = blocks.astype(F32).reshape(NX * NZL, 2 * TOK, HALF)
            halves.append(
                jnp.concatenate(
                    [
                        blocks[:, 0:TOK].reshape(ALL // 2, HALF),
                        blocks[:, TOK : 2 * TOK].reshape(ALL // 2, HALF),
                    ],
                    axis=1,
                )
            )
        rows = jnp.concatenate(halves, axis=0)
        sq = rows * rows
        ssq[...] += (sq[:, 0:128] + sq[:, 128:256]) + (sq[:, 256:384] + sq[:, 384:512])
        at = pl.ds(pl.multiple_of(i * PART, PART), PART)
        rows = (rows * gain_ref[:, at]).astype(BF16)
        acc[...] += jnp.dot(rows, wgu_v[at, :], preferred_element_type=F32)
        return 0

    lax.fori_loop(0, N_P, up_step, 0)
    spread = jnp.sum(ssq[...], -1, keepdims=True) * (1.0 / D)
    norm = lax.rsqrt(spread + 1e-06)
    coefs = rt[...].reshape(ALL, 128)
    lane = lax.broadcasted_iota(jnp.int32, (ALL, 128), 1)
    for j in range(2):
        coef = jnp.sum(jnp.where(lane == 2 * me + j, coefs, 0.0), -1, keepdims=True)
        gate = acc[:, 256 * j : 256 * j + 128] * norm
        up = acc[:, 256 * j + 128 : 256 * j + 256] * norm
        inner = gate / (1.0 + jnp.exp(-gate)) * up
        act[:, 128 * j : 128 * j + 128] = (inner * coef).astype(BF16)

    for cp in wd_cp:
        cp.wait()

    def down_step(i, _):
        yy, zz = lax.div(i, NZH), lax.rem(i, NZH)
        zs = pl.ds(pl.multiple_of(zz * NZL, NZL), NZL)
        at = pl.ds(pl.multiple_of(i * PART, PART), PART)
        made = jnp.dot(act[...], wd_v[:, at], preferred_element_type=F32)
        made = made.reshape(2, NX * NZL, TOK, PART)
        made = jnp.concatenate([made[..., 0:HALF], made[..., HALF:PART]], axis=2)
        made = made.astype(BF16).reshape(2, NX, NZL, 2 * TOK, HALF)
        p_buf[0, :, yy, zs] = made[0]
        p_buf[1, yy, :, zs] = made[1]
        return 0

    lax.fori_loop(0, N_P, down_step, 0)

    order = (2, 1, 3, 0)
    c_cp = []
    for k in order:
        j = lax.rem(sib_ia + k, 4)
        c_cp.append(send(p_buf.at[1 - core, j], s_buf.at[j], sibling))
    for cp, k in zip(c_cp, order):
        cp.wait_recv()
        j = lax.rem(ia + k, 4)
        m_buf[j] = (p_buf[core, j].astype(F32) + s_buf[j].astype(F32)).astype(BF16)

    def ring_sum(ref, i, n, at, arrive, mid):
        half = n // 2
        lo, hi = pl.ds(0, half), pl.ds(half, half)
        left, right, far = lax.rem(i + 3, 4), lax.rem(i + 1, 4), lax.rem(i + 2, 4)
        c_a = send(ref.at[far, lo], arrive.at[0], at(1))
        c_b = send(ref.at[far, hi], arrive.at[1], at(3))
        c_c = send(ref.at[right, hi], arrive.at[2], at(1))
        c_d = send(ref.at[left, lo], arrive.at[3], at(3))
        c_a.wait_recv()
        mid[0] = (ref[right, lo].astype(F32) + arrive[0].astype(F32)).astype(BF16)
        c_e = send(mid.at[0], arrive.at[4], at(1))
        c_b.wait_recv()
        mid[1] = (ref[left, hi].astype(F32) + arrive[1].astype(F32)).astype(BF16)
        c_f = send(mid.at[1], arrive.at[5], at(3))
        c_d.wait_recv()
        c_e.wait_recv()
        low = ref[i, lo].astype(F32) + arrive[3].astype(F32) + arrive[4].astype(F32)
        c_c.wait_recv()
        c_f.wait_recv()
        high = ref[i, hi].astype(F32) + arrive[2].astype(F32) + arrive[5].astype(F32)
        return low, high

    low, high = ring_sum(m_buf, ia, 4, at_a, a_in, a_mid)
    n_buf[0:2] = low.astype(BF16)
    n_buf[2:4] = high.astype(BF16)
    low, high = ring_sum(n_buf, ib, N_Z, at_b, b_in, b_mid)
    n2_buf[0:4] = low
    n2_buf[4:8] = high
    z_send[...] = n2_buf[...].astype(BF16)
    z_cp = [
        send(z_send.at[lax.rem(z + k, N_Z)], z_recv.at[k], at_z(k)) for k in range(1, N_Z)
    ]
    result = hid[...] + n2_buf[z]
    for k in range(1, N_Z):
        z_cp[k - 1].wait_recv()
        result = result + z_recv[k].astype(F32)
    o_s[...] = unpacked(result)
    for s in range(2):
        out_ref[s] = o_s[REQS * s : REQS * (s + 1), :].astype(BF16)
    guest_cp.wait_recv()
    for cp in sent:
        cp.wait_send()


def shards(
    queries,
    fresh_entries,
    cache_blocks,
    lengths,
    migration,
    residual,
    out_weight,
    norm_gain,
    routes,
    route_gates,
    w_gate,
    w_up,
    w_down,
):
    vmem = pl.BlockSpec(memory_space=pltpu.VMEM)
    smem = pl.BlockSpec(memory_space=pltpu.SMEM)
    hbm = pl.BlockSpec(memory_space=pl.ANY)
    block = (2 * TOK, HALF)

    def buf(*shape, dtype=BF16):
        return pltpu.VMEM(shape, dtype)

    return pl.pallas_call(
        kernel,
        out_shape=(
            jax.ShapeDtypeStruct((2, REQS, PART), BF16),
            jax.ShapeDtypeStruct((8, ROWS, 512), BF16),
        ),
        in_specs=[vmem, vmem, hbm, smem, smem, vmem, hbm, vmem, vmem, vmem, hbm, hbm, hbm],
        out_specs=(vmem, hbm),
        scratch_shapes=[
            buf(REQS, BLOCKS, ROWS, 512),
            buf(PART, D),
            buf(D, 512),
            buf(256, D),
            buf(8, ROWS, 512),
            buf(TOK, D, dtype=F32),
            buf(QH * TOK, HD),
            buf(2, 2, TOK, HD, dtype=F32),
            buf(TOK, PART, dtype=F32),
            buf(N_P, OWN * TOK + 16, HD),
            buf(N_P, OWN * TOK + 16, HD),
            buf(N_P, *block),
            buf(N_P, *block),
            buf(*block, dtype=F32),
            buf(2, NX, NZL, TOK, 128, dtype=F32),
            buf(2, 4, 4, N_Z, *block),
            buf(ALL, 512, dtype=F32),
            buf(ALL, 128, dtype=F32),
            buf(ALL, 256),
            buf(2, 4, 4, N_Z, *block),
            buf(4, 4, N_Z, *block),
            buf(4, 4, N_Z, *block),
            buf(6, 2, N_Z, *block),
            buf(2, 2, N_Z, *block),
            buf(4, N_Z, *block),
            buf(6, N_Z // 2, *block),
            buf(2, N_Z // 2, *block),
            buf(N_Z, *block, dtype=F32),
            buf(N_Z, *block),
            buf(N_Z, *block),
            buf(TOK, PART, dtype=F32),
            pltpu.SemaphoreType.DMA((16,)),
            pltpu.SemaphoreType.DMA((N_SEMS,)),
            pltpu.SemaphoreType.DMA((N_SEMS,)),
        ],
        compiler_params=pltpu.CompilerParams(
            collective_id=0, has_side_effects=True, vmem_limit_bytes=48 * MIB
        ),
        cost_estimate=pl.CostEstimate(
            flops=2_000_000_000, bytes_accessed=13 * MIB, transcendentals=200_000
        ),
    )(
        queries,
        fresh_entries,
        cache_blocks,
        lengths,
        migration,
        residual,
        out_weight,
        norm_gain.reshape(1, D),
        routes,
        route_gates,
        w_gate,
        w_up,
        w_down,
    )


def solution(mesh):
    in_specs = (
        P(None, "dp", None),
        P(None, "dp", None),
        P("dp", None, "expert", None),
        P("dp"),
        P("dp", None),
        P(None, "dp", None),
        P("expert", None),
        P(),
        P(None, "dp", None),
        P(None, "dp", None),
        P("dp", None, "expert"),
        P("dp", None, "expert"),
        P("dp", "expert", None),
    )
    out_specs = (P(None, "dp", "expert"), P("dp", "expert", None))
    return jax.shard_map(shards, mesh=mesh, in_specs=in_specs, out_specs=out_specs, check_vma=False)
```

```python
import functools
import math

import jax
import jax.numpy as jnp
from jax import lax
from jax.experimental import pallas as pl
from jax.experimental.pallas import tpu as pltpu
from jax.sharding import PartitionSpec as P

MESH = pl.DeviceIdType.MESH
HD = 128
QH = 32
KVH = 2
TOPK = 8
BLOCKS = 32
NX, NZL, NY, NZH = 4, 4, 4, 2
N_P = NY * NZH
N_Z = NZH * NZL
N_DP = NX * NZL * 2
REQS = 4
TOK = 2 * REQS
D = 4096
PART = D // N_P
HALF = PART // 2
PAIR = 2 * PART
FAR_Z = (4, 3, 5, 2, 6, 1, 7)
FAR_P = (3, 5, 1, 7, 4, 2, 6)
ROWS = 16
POSN = BLOCKS * ROWS
OWN = QH // N_P
ALL = N_DP * TOK
F32 = jnp.float32
BF16 = jnp.bfloat16
NEG = -1e30
N_SEMS = 88
MIB = 1024 * 1024


def kernel(
    q_ref,
    fresh_ref,
    cache_ref,
    len_ref,
    mig_ref,
    res_ref,
    ow_ref,
    gain_ref,
    routes_ref,
    gates_ref,
    wg_ref,
    wu_ref,
    wd_ref,
    out_ref,
    guest_ref,
    q_v,
    fresh_v,
    len_v,
    mig_s,
    res_v,
    gain_v,
    routes_v,
    gates_v,
    cache_v,
    ow_v,
    wgu_v,
    wd_v,
    picked_v,
    q_s,
    q_b,
    f_s,
    r_s,
    a_send,
    a_recv,
    b_send,
    b_recv,
    zr,
    hid,
    rt,
    g_buf,
    rows_v,
    ssq,
    act,
    p_buf,
    s_buf,
    m_buf,
    a_in,
    n_buf,
    b_in,
    n2_buf,
    z_send,
    z_recv,
    o_s,
    load_sem,
    send_sem,
    recv_sem,
):
    me = lax.axis_index("dp")
    p = lax.axis_index("expert")
    core = lax.rem(me, 2)
    zlo = lax.rem(lax.div(me, 2), NZL)
    x = lax.div(me, 2 * NZL)
    y = lax.div(p, NZH)
    zhi = lax.rem(p, NZH)
    z = zhi * NZL + zlo

    def place(x_, y_, zlo_, zhi_, core_):
        return ((x_ * NZL + zlo_) * 2 + core_, y_ * NZH + zhi_)

    def at_p(k):
        return (me, lax.rem(p + k, N_P))

    def at_y(k):
        return place(x, lax.rem(y + k, NY), zlo, zhi, core)

    def at_z(k):
        t = lax.rem(z + k, N_Z)
        return place(x, y, lax.rem(t, NZL), lax.div(t, NZL), core)

    def at_x(k):
        return place(lax.rem(x + k, NX), y, zlo, zhi, core)

    def at_zlo(k):
        return place(x, y, lax.rem(zlo + k, NZL), zhi, core)

    def at_a(k):
        return place(lax.rem(x + (1 - core) * k, NX), lax.rem(y + core * k, NY), zlo, zhi, core)

    def at_b(k):
        return place(lax.rem(x + core * k, NX), lax.rem(y + (1 - core) * k, NY), zlo, zhi, core)

    sibling = place(x, y, zlo, zhi, 1 - core)
    ia = (1 - core) * x + core * y
    ib = core * x + (1 - core) * y
    sib_ib = ia

    loads = []

    def load(src, dst):
        cp = pltpu.make_async_copy(src, dst, load_sem.at[len(loads)])
        cp.start()
        loads.append(cp)
        return cp

    small_cp = [load(routes_ref, routes_v), load(gates_ref, gates_v), load(q_ref, q_v)]
    len_cp = load(len_ref, len_v)
    mig_cp = load(mig_ref, mig_s)
    cache_cp = [load(cache_ref.at[r], cache_v.at[r]) for r in range(REQS)]
    fresh_cp = load(fresh_ref, fresh_v)
    res_cp = load(res_ref, res_v)
    gain_cp = load(gain_ref, gain_v)
    ow_cp = load(ow_ref, ow_v)
    w_cp = []
    for j in range(2):
        w_cp.append(load(wg_ref.at[j], wgu_v.at[:, pl.ds(256 * j, 128)]))
        w_cp.append(load(wu_ref.at[j], wgu_v.at[:, pl.ds(256 * j + 128, 128)]))
    wd_cp = [load(wd_ref.at[j], wd_v.at[pl.ds(128 * j, 128)]) for j in range(2)]

    barrier = pltpu.get_barrier_semaphore()
    peers = [at_p(k) for k in range(1, N_P)]
    peers += [at_z(k) for k in range(1, N_Z) if k != NZL]
    peers += [at_x(k) for k in range(1, NX)]
    peers += [sibling]
    for peer in peers:
        pl.semaphore_signal(barrier, inc=1, device_id=peer, device_id_type=MESH)

    sent = []

    def send(src, dst, peer):
        k = len(sent)
        cp = pltpu.make_async_remote_copy(
            src_ref=src,
            dst_ref=dst,
            send_sem=send_sem.at[k],
            recv_sem=recv_sem.at[k],
            device_id=peer,
            device_id_type=MESH,
        )
        cp.start()
        sent.append(cp)
        return cp

    for cp in small_cp:
        cp.wait()

    lane = lax.broadcasted_iota(jnp.int32, (REQS, 128), 1)
    for s in range(2):
        ids = routes_v[s]
        vals = gates_v[s]
        coef = jnp.zeros((REQS, 128), F32)
        for k in range(TOPK):
            coef = coef + jnp.where(lane == ids[:, k : k + 1], vals[:, k : k + 1], 0.0)
        rt[core, x, zlo, pl.ds(REQS * s, REQS), :] = coef

    for s in range(2):
        q_s[pl.ds(REQS * s, REQS), :] = q_v[s].astype(F32)
    q_b[...] = jnp.concatenate(
        [q_s[:, h * HD : (h + 1) * HD] for h in range(QH)], axis=0
    ).astype(BF16)

    mig_cp.wait()
    len_cp.wait()
    for cp in cache_cp:
        cp.wait()
    for m in range(8):
        picked_v[m] = cache_v[mig_s[0, m], mig_s[1, m]]

    scale = 1.0 / math.sqrt(HD)
    col = lax.broadcasted_iota(jnp.int32, (TOK, POSN), 1)
    row = lax.rem(lax.broadcasted_iota(jnp.int32, (TOK, POSN), 0), REQS)
    position = lax.div(col, ROWS) * (ROWS * N_P) + p * ROWS + lax.rem(col, ROWS)
    limit = jnp.full((TOK, POSN), 0, jnp.int32)
    for r in range(REQS):
        limit = jnp.where(row == r, len_v[0:1, r : r + 1], limit)
    valid = position < limit
    hk = QH // KVH * TOK
    rid = lax.rem(lax.broadcasted_iota(jnp.int32, (hk, POSN), 0), REQS)
    rid_o = lax.rem(lax.broadcasted_iota(jnp.int32, (hk, HD), 0), REQS)
    sub = lax.broadcasted_iota(jnp.int32, (OWN * TOK, 128), 0)
    lan = lax.broadcasted_iota(jnp.int32, (OWN * TOK, 128), 1)
    for k in range(KVH):
        qk = q_b[k * hk : (k + 1) * hk]
        scores = None
        for r in range(REQS):
            keys = cache_v[r, :, :, k * HD : (k + 1) * HD].reshape(POSN, HD)
            part = lax.dot_general(
                qk, keys, (((1,), (1,)), ((), ())), preferred_element_type=F32
            )
            scores = part if r == 0 else jnp.where(rid == r, part, scores)
        scores = scores.reshape(hk // TOK, TOK, POSN)
        scores = jnp.where(valid[None], scores * scale, NEG)
        peak = jnp.max(scores, -1, keepdims=True).astype(BF16).astype(F32)
        weights = jnp.exp(scores - peak)
        total = jnp.sum(weights, -1, keepdims=True)
        weights = weights.reshape(hk, POSN).astype(BF16)
        state = None
        for r in range(REQS):
            vals = cache_v[r, :, :, (KVH + k) * HD : (KVH + k + 1) * HD].reshape(POSN, HD)
            part = jnp.dot(weights, vals, preferred_element_type=F32)
            state = part if r == 0 else jnp.where(rid_o == r, part, state)
        peak = peak.reshape(hk, 1)
        total = total.reshape(hk, 1)
        total_hi = total.astype(BF16).astype(F32)
        total_lo = total - total_hi
        n_rows = OWN * TOK
        for i in range(hk // n_rows):
            dest = k * (hk // n_rows) + i
            rows = slice(i * n_rows, (i + 1) * n_rows)
            a_send[dest, 0:n_rows, :] = state[rows].astype(BF16)
            stat = jnp.where(lan == sub, peak[rows], 0.0)
            stat = jnp.where(lan == sub + n_rows, total_hi[rows], stat)
            stat = jnp.where(lan == sub + 2 * n_rows, total_lo[rows], stat)
            stat = jnp.sum(stat, axis=0, keepdims=True)
            a_send[dest, n_rows : n_rows + 16, :] = jnp.broadcast_to(stat, (16, 128)).astype(BF16)

    pl.semaphore_wait(barrier, len(peers))

    a_cp = []
    for k in FAR_P:
        a_cp.append(send(a_send.at[lax.rem(p + k, N_P)], a_recv.at[k], at_p(k)))
    rt_cp = [
        send(rt.at[core, x, zlo], rt.at[core, x, zlo], at_zlo(k)) for k in range(1, NZL)
    ]
    guest_cp = send(picked_v, guest_ref, at_x(2))
    a_recv[0] = a_send[p]

    fresh_cp.wait()
    kv = lax.div(p, N_P // KVH)
    for n in range(2):
        for j in range(2):
            new = fresh_v[
                n, :, pl.ds(pl.multiple_of((j * KVH + kv) * HD, HD), HD)
            ].astype(F32)
            f_s[n, j, 0:REQS, :] = new
            f_s[n, j, REQS:TOK, :] = new
    q_own = q_s[:, pl.ds(pl.multiple_of(p * PART, PART), PART)]
    q_own = jnp.stack([q_own[:, i * HD : (i + 1) * HD] for i in range(OWN)], axis=0)
    f_scores = [
        jnp.sum(q_own * f_s[n, 0][None], -1, keepdims=True) * scale for n in range(2)
    ]
    step_row = lax.broadcasted_iota(jnp.int32, (OWN, TOK, 1), 1)
    f_scores[1] = jnp.where(step_row >= REQS, f_scores[1], NEG)

    for cp in a_cp:
        cp.wait_recv()
    n_rows = OWN * TOK

    def to_row(v):
        return jnp.sum(jnp.where(lan == sub, v, 0.0), axis=0, keepdims=True)

    def to_col(v):
        return jnp.sum(jnp.where(lan == sub, v, 0.0), axis=1, keepdims=True)

    stat = jnp.concatenate(
        [a_recv[k, n_rows : n_rows + 16, :].astype(F32)[0:1] for k in range(N_P)], axis=0
    )
    totals = pltpu.roll(stat, 128 - n_rows, 1) + pltpu.roll(stat, 128 - 2 * n_rows, 1)
    f_scores = [to_row(f.reshape(n_rows, 1)) for f in f_scores]
    top = jnp.maximum(jnp.max(stat, axis=0, keepdims=True), jnp.maximum(f_scores[0], f_scores[1]))
    used = lan[0:1] < n_rows
    w_dev = jnp.exp(jnp.where(used, stat - top, NEG))
    w_new = [jnp.exp(jnp.where(used, f - top, NEG)) for f in f_scores]
    denom = jnp.sum(w_dev * totals, axis=0, keepdims=True) + w_new[0] + w_new[1]
    denom = 1.0 / jnp.where(used, denom, 1.0)
    w_dev = w_dev * denom
    numer = jnp.zeros((n_rows, HD), F32)
    for n in range(2):
        vals = jnp.broadcast_to(f_s[n, 1][None], (OWN, TOK, HD)).reshape(n_rows, HD)
        numer = numer + to_col(w_new[n] * denom) * vals
    for k in range(N_P):
        numer = numer + to_col(w_dev[k : k + 1]) * a_recv[k, 0:n_rows, :].astype(F32)
    attention = numer.reshape(OWN, TOK, HD)
    attention = jnp.concatenate([attention[i] for i in range(OWN)], axis=1).astype(BF16)

    for cp in rt_cp:
        cp.wait_recv()
    rt_cp = [send(rt.at[core, x], rt.at[core, x], at_x(k)) for k in range(1, NX)]

    def packed(v):
        half = v.shape[1] // 2
        return jnp.concatenate([v[:, 0:half], v[:, half:]], axis=0)

    def unpacked(v):
        return jnp.concatenate([v[0:TOK], v[TOK : 2 * TOK]], axis=1)

    res_cp.wait()
    at = pl.ds(pl.multiple_of(y * PAIR, PAIR), PAIR)
    for s in range(2):
        r_s[pl.ds(REQS * s, REQS), :] = res_v[s, :, at].astype(F32)
    ow_cp.wait()
    b_cp = []
    for k in (2, 1, 3, 0):
        yy = lax.rem(y + k, NY)
        term = jnp.dot(
            attention,
            ow_v[:, pl.ds(pl.multiple_of(yy * PAIR, PAIR), PAIR)],
            preferred_element_type=F32,
        )
        if k != 0:
            b_send[k] = packed(term).astype(BF16)
            b_cp.append(send(b_send.at[k], b_recv.at[k], at_y(k)))
    hidden = packed(jnp.where(zhi == 0, r_s[...], 0.0) + term)
    for k, cp in zip((2, 1, 3), b_cp):
        cp.wait_recv()
        hidden = hidden + b_recv[k].astype(F32)
    zr[z] = hidden.astype(BF16)

    z_cp = [send(zr.at[z], zr.at[z], at_z(k)) for k in FAR_Z]
    for cp in rt_cp:
        cp.wait_recv()
    rt_cp = [send(rt.at[core], rt.at[core], sibling)]
    for cp in z_cp:
        cp.wait_recv()
    for t in range(NZL):
        hidden = zr[t].astype(F32) + zr[NZL + t].astype(F32)
        g_buf[core, ia, ib, t] = hidden.astype(BF16)
    hidden = zr[zlo].astype(F32) + zr[NZL + zlo].astype(F32)
    hid[0] = hidden[0:TOK]
    hid[1] = hidden[TOK : 2 * TOK]

    def to_ring(jb):
        piece = g_buf.at[core, ia, jb]
        return [send(piece, piece, at_a(k)) for k in (2, 1, 3)]

    mine = g_buf.at[core, ia, ib]
    b_cp = {k: send(mine, mine, at_b(k)) for k in (2, 1, 3)}
    a_cp = [to_ring(ib)]
    for k in (1, 3, 2):
        b_cp[k].wait_recv()
        a_cp.append(to_ring(lax.rem(ib + 4 - k, 4)))

    gain_cp.wait()
    ssq[...] = jnp.zeros_like(ssq)

    def prepare(plane, jb):
        def step(ja, _):
            xx = (1 - plane) * ja + plane * jb
            yy = plane * ja + (1 - plane) * jb
            blocks = g_buf[plane, ja, jb].astype(F32)
            rows = jnp.concatenate(
                [
                    blocks[:, 0:TOK].reshape(NZL * TOK, PART),
                    blocks[:, TOK : 2 * TOK].reshape(NZL * TOK, PART),
                ],
                axis=1,
            )
            sq = rows * rows
            while sq.shape[1] > 128:
                half = sq.shape[1] // 2
                sq = sq[:, 0:half] + sq[:, half:]
            at_row = pl.ds(pl.multiple_of(plane * (ALL // 2) + xx * (NZL * TOK), NZL * TOK), NZL * TOK)
            at_col = pl.ds(pl.multiple_of(yy * PAIR, PAIR), PAIR)
            ssq[at_row, :] += sq
            rows_v[at_row, at_col] = (rows * gain_v[:, at_col]).astype(BF16)
            return 0

        lax.fori_loop(0, 4, step, 0)

    def across(ja, jb):
        piece = g_buf.at[core, ja, jb]
        return send(piece, piece, sibling)

    order = (0, 1, 3, 2)
    c_cp = [[across(ia, lax.rem(ib + 4 - k, 4))] for k in order]
    for i, k in enumerate(order):
        jb = lax.rem(ib + 4 - k, 4)
        for ka, cp in zip((2, 1, 3), a_cp[i]):
            cp.wait_recv()
            c_cp[i].append(across(lax.rem(ia + 4 - ka, 4), jb))
        prepare(core, jb)
        if i > 0:
            for cp in c_cp[i - 1]:
                cp.wait_recv()
            prepare(1 - core, lax.rem(sib_ib + 4 - order[i - 1], 4))
    for cp in c_cp[3]:
        cp.wait_recv()
    prepare(1 - core, lax.rem(sib_ib + 4 - order[3], 4))
    for cp in rt_cp:
        cp.wait_recv()

    for cp in w_cp:
        cp.wait()
    spread = jnp.sum(ssq[...], -1, keepdims=True) * (1.0 / D)
    norm = lax.rsqrt(spread + 1e-06)
    coefs = rt[...].reshape(ALL, 128)
    lane = lax.broadcasted_iota(jnp.int32, (ALL, 128), 1)
    for j in range(2):
        coef = jnp.sum(jnp.where(lane == 2 * me + j, coefs, 0.0), -1, keepdims=True)
        both = jnp.dot(
            rows_v[...], wgu_v[:, 256 * j : 256 * j + 256], preferred_element_type=F32
        )
        gate = both[:, 0:128] * norm
        up = both[:, 128:256] * norm
        inner = gate / (1.0 + jnp.exp(-gate)) * up
        act[:, 128 * j : 128 * j + 128] = (inner * coef).astype(BF16)

    for cp in wd_cp:
        cp.wait()

    def down_step(yy, _):
        at = pl.ds(pl.multiple_of(yy * PAIR, PAIR), PAIR)
        made = jnp.dot(act[...], wd_v[:, at], preferred_element_type=F32)
        made = made.reshape(2, NX * NZL, TOK, PAIR)
        made = jnp.concatenate([made[..., 0:PART], made[..., PART:PAIR]], axis=2)
        made = made.astype(BF16).reshape(2, NX, NZL, 2 * TOK, PART)
        p_buf[0, :, yy] = made[0]
        p_buf[1, yy] = made[1]
        return 0

    lax.fori_loop(0, NY, down_step, 0)

    order = (2, 1, 3, 0)
    c_cp = []
    for k in order:
        jb = lax.rem(sib_ib + k, 4)
        c_cp.append(send(p_buf.at[1 - core, :, jb], s_buf.at[:, jb], sibling))
    a_cp = []
    for i, k in enumerate(order):
        c_cp[i].wait_recv()
        jb = lax.rem(ib + k, 4)
        m_buf[:, jb] = (p_buf[core, :, jb].astype(F32) + s_buf[:, jb].astype(F32)).astype(BF16)
        a_cp.append(
            [
                send(m_buf.at[lax.rem(ia + ka, 4), jb], a_in.at[i, ka], at_a(ka))
                for ka in (2, 1, 3)
            ]
        )
    b_cp = []
    for i, k in enumerate(order):
        for cp in a_cp[i]:
            cp.wait_recv()
        jb = lax.rem(ib + k, 4)
        total = m_buf[ia, jb].astype(F32)
        for ka in range(1, 4):
            total = total + a_in[i, ka].astype(F32)
        if k != 0:
            n_buf[k] = total.astype(BF16)
            b_cp.append(send(n_buf.at[k], b_in.at[k], at_b(k)))
    for k, cp in zip(order, b_cp):
        cp.wait_recv()
        total = total + b_in[k].astype(F32)
    for t in range(NZL):
        n2_buf[t] = packed(total[t, 0:TOK])
        n2_buf[NZL + t] = packed(total[t, TOK : 2 * TOK])
    z_send[...] = n2_buf[...].astype(BF16)
    z_cp = [send(z_send.at[lax.rem(z + k, N_Z)], z_recv.at[k], at_z(k)) for k in FAR_Z]
    result = packed(hid[zhi]) + n2_buf[z]
    for k, cp in zip(FAR_Z, z_cp):
        cp.wait_recv()
        result = result + z_recv[k].astype(F32)
    o_s[...] = unpacked(result)
    for s in range(2):
        out_ref[s] = o_s[REQS * s : REQS * (s + 1), :].astype(BF16)
    guest_cp.wait_recv()
    for cp in sent:
        cp.wait_send()


def finish_kernel(a_ref, b_ref, a_out, b_out, a_v, b_v, sem):
    pairs = [(a_ref, a_v), (b_ref, b_v), (a_v, a_out), (b_v, b_out)]
    copies = [pltpu.make_async_copy(*pair, sem.at[i]) for i, pair in enumerate(pairs)]
    copies[0].start()
    copies[1].start()
    for i in range(2):
        copies[i].wait()
        copies[i + 2].start()
    for i in range(2):
        copies[i + 2].wait()


def shards(
    queries,
    fresh_entries,
    cache_blocks,
    lengths,
    migration,
    residual,
    out_weight,
    norm_gain,
    routes,
    route_gates,
    w_gate,
    w_up,
    w_down,
):
    vmem = pl.BlockSpec(memory_space=pltpu.VMEM)
    hbm = pl.BlockSpec(memory_space=pltpu.HBM)
    pair = (2 * TOK, PART)
    block = (2 * TOK, HALF)

    def buf(*shape, dtype=BF16):
        return pltpu.VMEM(shape, dtype)

    shapes = (
        jax.ShapeDtypeStruct((2, REQS, PART), BF16),
        jax.ShapeDtypeStruct((8, ROWS, 512), BF16),
    )
    made = pl.pallas_call(
        kernel,
        out_shape=shapes,
        in_specs=[hbm] * 13,
        out_specs=(vmem, hbm),
        scratch_shapes=[
            buf(2, REQS, D),
            buf(2, REQS, 512),
            buf(1, REQS, dtype=jnp.int32),
            pltpu.SMEM((2, 8), jnp.int32),
            buf(2, REQS, D),
            buf(1, D, dtype=F32),
            buf(2, REQS, TOPK, dtype=jnp.int32),
            buf(2, REQS, TOPK, dtype=F32),
            buf(REQS, BLOCKS, ROWS, 512),
            buf(PART, D),
            buf(D, 512),
            buf(256, D),
            buf(8, ROWS, 512),
            buf(TOK, D, dtype=F32),
            buf(QH * TOK, HD),
            buf(2, 2, TOK, HD, dtype=F32),
            buf(TOK, PAIR, dtype=F32),
            buf(N_P, OWN * TOK + 16, HD),
            buf(N_P, OWN * TOK + 16, HD),
            buf(NY, *pair),
            buf(NY, *pair),
            buf(N_Z, *pair),
            buf(2, TOK, PART, dtype=F32),
            buf(2, NX, NZL, TOK, 128, dtype=F32),
            buf(2, 4, 4, NZL, *pair),
            buf(ALL, D),
            buf(ALL, 128, dtype=F32),
            buf(ALL, 256),
            buf(2, 4, 4, NZL, *pair),
            buf(4, 4, NZL, *pair),
            buf(4, 4, NZL, *pair),
            buf(4, 4, NZL, *pair),
            buf(4, NZL, *pair),
            buf(4, NZL, *pair),
            buf(N_Z, *block, dtype=F32),
            buf(N_Z, *block),
            buf(N_Z, *block),
            buf(TOK, PART, dtype=F32),
            pltpu.SemaphoreType.DMA((24,)),
            pltpu.SemaphoreType.DMA((N_SEMS,)),
            pltpu.SemaphoreType.DMA((N_SEMS,)),
        ],
        compiler_params=pltpu.CompilerParams(
            collective_id=0, has_side_effects=True, vmem_limit_bytes=60 * MIB
        ),
        cost_estimate=pl.CostEstimate(
            flops=2_000_000_000, bytes_accessed=13 * MIB, transcendentals=200_000
        ),
    )(
        queries,
        fresh_entries,
        cache_blocks,
        lengths.reshape(1, REQS),
        migration.T,
        residual,
        out_weight,
        norm_gain.reshape(1, D),
        routes,
        route_gates,
        w_gate,
        w_up,
        w_down,
    )
    return pl.pallas_call(
        finish_kernel,
        out_shape=shapes,
        in_specs=[hbm] * 2,
        out_specs=(hbm, hbm),
        scratch_shapes=[
            buf(2, REQS, PART),
            buf(8, ROWS, 512),
            pltpu.SemaphoreType.DMA((4,)),
        ],
        compiler_params=pltpu.CompilerParams(vmem_limit_bytes=60 * MIB),
    )(*made)


def solution(mesh):
    in_specs = (
        P(None, "dp", None),
        P(None, "dp", None),
        P("dp", None, "expert", None),
        P("dp"),
        P("dp", None),
        P(None, "dp", None),
        P("expert", None),
        P(),
        P(None, "dp", None),
        P(None, "dp", None),
        P("dp", None, "expert"),
        P("dp", None, "expert"),
        P("dp", "expert", None),
    )
    out_specs = (P(None, "dp", "expert"), P("dp", "expert", None))
    return jax.shard_map(shards, mesh=mesh, in_specs=in_specs, out_specs=out_specs, check_vma=False)
```

```python
import functools
import math

import jax
import jax.numpy as jnp
from jax import lax
from jax.experimental import pallas as pl
from jax.experimental.pallas import tpu as pltpu
from jax.sharding import PartitionSpec as P

MESH = pl.DeviceIdType.MESH
HD = 128
QH = 32
KVH = 2
TOPK = 8
BLOCKS = 32
NX, NZL, NY, NZH = 4, 4, 4, 2
N_P = NY * NZH
N_Z = NZH * NZL
N_DP = NX * NZL * 2
REQS = 4
TOK = 2 * REQS
D = 4096
PART = D // N_P
HALF = PART // 2
PAIR = 2 * PART
Z_LABELS = (5, 6, 2, 1, 4, 3, 7)
OFFSETS = ((2, 1), (3, 0))
SLOT = {2: 0, 1: 1, 3: 2, 0: 3}
FAR_P = (3, 5, 1, 7, 4, 2, 6)
ROWS = 16
POSN = BLOCKS * ROWS
OWN = QH // N_P
ALL = N_DP * TOK
F32 = jnp.float32
BF16 = jnp.bfloat16
NEG = -1e30
N_SEMS = 180
MIB = 1024 * 1024


def kernel(
    q_ref,
    fresh_ref,
    cache_ref,
    len_ref,
    mig_ref,
    res_ref,
    ow_ref,
    gain_ref,
    routes_ref,
    gates_ref,
    wg_ref,
    wu_ref,
    wd_ref,
    out_ref,
    guest_ref,
    q_v,
    fresh_v,
    len_v,
    mig_s,
    res_v,
    gain_v,
    routes_v,
    gates_v,
    cache_v,
    ow_v,
    wgu_v,
    wd_v,
    picked_v,
    q_s,
    q_b,
    f_s,
    r_s,
    a_send,
    a_recv,
    b_send,
    b_recv,
    zr,
    hid,
    rt,
    g_buf,
    rows_v,
    ssq,
    act,
    p_buf,
    s_buf,
    m_buf,
    a_in,
    n_buf,
    t_buf,
    e_send,
    e_recv,
    o_s,
    load_sem,
    send_sem,
    recv_sem,
):
    me = lax.axis_index("dp")
    p = lax.axis_index("expert")
    core = lax.rem(me, 2)
    zlo = lax.rem(lax.div(me, 2), NZL)
    x = lax.div(me, 2 * NZL)
    y = lax.div(p, NZH)
    zhi = lax.rem(p, NZH)
    z = zhi * NZL + zlo

    def place(x_, y_, zlo_, zhi_, core_):
        return ((x_ * NZL + zlo_) * 2 + core_, y_ * NZH + zhi_)

    def at_p(k):
        return (me, lax.rem(p + k, N_P))

    def at_y(k):
        return place(x, lax.rem(y + k, NY), zlo, zhi, core)

    def at_z(k):
        t = lax.rem(z + k, N_Z)
        return place(x, y, lax.rem(t, NZL), lax.div(t, NZL), core)

    def at_x(k):
        return place(lax.rem(x + k, NX), y, zlo, zhi, core)

    def at_zlo(k):
        return place(x, y, lax.rem(zlo + k, NZL), zhi, core)

    def at_a(k):
        return place(lax.rem(x + (1 - core) * k, NX), lax.rem(y + core * k, NY), zlo, zhi, core)

    def at_b(k):
        return place(lax.rem(x + core * k, NX), lax.rem(y + (1 - core) * k, NY), zlo, zhi, core)

    def at_bz(kb, kz):
        t = lax.rem(z + kz, N_Z)
        return place(
            lax.rem(x + core * kb, NX),
            lax.rem(y + (1 - core) * kb, NY),
            lax.rem(t, NZL),
            lax.div(t, NZL),
            core,
        )

    sibling = place(x, y, zlo, zhi, 1 - core)
    ia = (1 - core) * x + core * y
    ib = core * x + (1 - core) * y
    sib_ib = ia
    sib_ia = ib

    barrier = pltpu.get_barrier_semaphore()
    peers = [at_p(k) for k in range(1, N_P)]
    peers += [at_z(k) for k in range(1, N_Z) if k != NZL]
    peers += [at_x(k) for k in range(1, NX)]
    peers += [at_bz(kb, kz) for kb in range(1, 4) for kz in range(1, N_Z)]
    peers += [sibling]
    for peer in peers:
        pl.semaphore_signal(barrier, inc=1, device_id=peer, device_id_type=MESH)

    loads = []

    def load(src, dst):
        cp = pltpu.make_async_copy(src, dst, load_sem.at[len(loads)])
        cp.start()
        loads.append(cp)
        return cp

    small_cp = [load(routes_ref, routes_v), load(gates_ref, gates_v), load(q_ref, q_v)]
    len_cp = load(len_ref, len_v)
    mig_cp = load(mig_ref, mig_s)
    cache_cp = [load(cache_ref.at[r], cache_v.at[r]) for r in range(REQS)]
    fresh_cp = load(fresh_ref, fresh_v)
    res_cp = load(res_ref, res_v)
    gain_cp = load(gain_ref, gain_v)
    sent = []

    def send(src, dst, peer):
        k = len(sent)
        cp = pltpu.make_async_remote_copy(
            src_ref=src,
            dst_ref=dst,
            send_sem=send_sem.at[k],
            recv_sem=recv_sem.at[k],
            device_id=peer,
            device_id_type=MESH,
        )
        cp.start()
        sent.append(cp)
        return cp

    for cp in small_cp:
        cp.wait()

    lane = lax.broadcasted_iota(jnp.int32, (REQS, 128), 1)
    for s in range(2):
        ids = routes_v[s]
        vals = gates_v[s]
        coef = jnp.zeros((REQS, 128), F32)
        for k in range(TOPK):
            coef = coef + jnp.where(lane == ids[:, k : k + 1], vals[:, k : k + 1], 0.0)
        rt[core, x, SLOT[0], pl.ds(REQS * s, REQS), :] = coef

    for s in range(2):
        q_s[pl.ds(REQS * s, REQS), :] = q_v[s].astype(F32)
    q_b[...] = jnp.concatenate(
        [q_s[:, h * HD : (h + 1) * HD] for h in range(QH)], axis=0
    ).astype(BF16)

    mig_cp.wait()
    len_cp.wait()
    for cp in cache_cp:
        cp.wait()
    ow_cp = load(ow_ref, ow_v)
    w_cp = []
    for j in range(2):
        w_cp.append(load(wg_ref.at[j], wgu_v.at[:, pl.ds(256 * j, 128)]))
        w_cp.append(load(wu_ref.at[j], wgu_v.at[:, pl.ds(256 * j + 128, 128)]))
    wd_cp = [load(wd_ref.at[j], wd_v.at[pl.ds(128 * j, 128)]) for j in range(2)]
    for m in range(8):
        picked_v[m] = cache_v[mig_s[0, m], mig_s[1, m]]

    scale = 1.0 / math.sqrt(HD)
    col = lax.broadcasted_iota(jnp.int32, (TOK, POSN), 1)
    row = lax.rem(lax.broadcasted_iota(jnp.int32, (TOK, POSN), 0), REQS)
    position = lax.div(col, ROWS) * (ROWS * N_P) + p * ROWS + lax.rem(col, ROWS)
    limit = jnp.full((TOK, POSN), 0, jnp.int32)
    for r in range(REQS):
        limit = jnp.where(row == r, len_v[0:1, r : r + 1], limit)
    valid = position < limit
    hk = QH // KVH * TOK
    rid = lax.rem(lax.broadcasted_iota(jnp.int32, (hk, POSN), 0), REQS)
    rid_o = lax.rem(lax.broadcasted_iota(jnp.int32, (hk, HD), 0), REQS)
    sub = lax.broadcasted_iota(jnp.int32, (OWN * TOK, 128), 0)
    lan = lax.broadcasted_iota(jnp.int32, (OWN * TOK, 128), 1)
    for k in range(KVH):
        qk = q_b[k * hk : (k + 1) * hk]
        scores = None
        for r in range(REQS):
            keys = cache_v[r, :, :, k * HD : (k + 1) * HD].reshape(POSN, HD)
            part = lax.dot_general(
                qk, keys, (((1,), (1,)), ((), ())), preferred_element_type=F32
            )
            scores = part if r == 0 else jnp.where(rid == r, part, scores)
        scores = scores.reshape(hk // TOK, TOK, POSN)
        scores = jnp.where(valid[None], scores * scale, NEG)
        peak = jnp.max(scores, -1, keepdims=True).astype(BF16).astype(F32)
        weights = jnp.exp(scores - peak)
        total = jnp.sum(weights, -1, keepdims=True)
        weights = weights.reshape(hk, POSN).astype(BF16)
        state = None
        for r in range(REQS):
            vals = cache_v[r, :, :, (KVH + k) * HD : (KVH + k + 1) * HD].reshape(POSN, HD)
            part = jnp.dot(weights, vals, preferred_element_type=F32)
            state = part if r == 0 else jnp.where(rid_o == r, part, state)
        peak = peak.reshape(hk, 1)
        total = total.reshape(hk, 1)
        total_hi = total.astype(BF16).astype(F32)
        total_lo = total - total_hi
        n_rows = OWN * TOK
        for i in range(hk // n_rows):
            dest = k * (hk // n_rows) + i
            rows = slice(i * n_rows, (i + 1) * n_rows)
            a_send[dest, 0:n_rows, :] = state[rows].astype(BF16)
            stat = jnp.where(lan == sub, peak[rows], 0.0)
            stat = jnp.where(lan == sub + n_rows, total_hi[rows], stat)
            stat = jnp.where(lan == sub + 2 * n_rows, total_lo[rows], stat)
            stat = jnp.sum(stat, axis=0, keepdims=True)
            a_send[dest, n_rows : n_rows + 16, :] = jnp.broadcast_to(stat, (16, 128)).astype(BF16)

    pl.semaphore_wait(barrier, len(peers))

    a_cp = []
    for k in FAR_P:
        a_cp.append(send(a_send.at[lax.rem(p + k, N_P)], a_recv.at[k], at_p(k)))
    rt_cp = [
        send(rt.at[core, x, SLOT[0]], rt.at[core, x, SLOT[k]], at_zlo(k))
        for k in range(1, NZL)
    ]
    guest_cp = send(picked_v, guest_ref, at_x(2))
    a_recv[0] = a_send[p]

    fresh_cp.wait()
    kv = lax.div(p, N_P // KVH)
    for n in range(2):
        for j in range(2):
            new = fresh_v[
                n, :, pl.ds(pl.multiple_of((j * KVH + kv) * HD, HD), HD)
            ].astype(F32)
            f_s[n, j, 0:REQS, :] = new
            f_s[n, j, REQS:TOK, :] = new
    q_own = q_s[:, pl.ds(pl.multiple_of(p * PART, PART), PART)]
    q_own = jnp.stack([q_own[:, i * HD : (i + 1) * HD] for i in range(OWN)], axis=0)
    f_scores = [
        jnp.sum(q_own * f_s[n, 0][None], -1, keepdims=True) * scale for n in range(2)
    ]
    step_row = lax.broadcasted_iota(jnp.int32, (OWN, TOK, 1), 1)
    f_scores[1] = jnp.where(step_row >= REQS, f_scores[1], NEG)

    for cp in a_cp:
        cp.wait_recv()
    n_rows = OWN * TOK

    def to_row(v):
        return jnp.sum(jnp.where(lan == sub, v, 0.0), axis=0, keepdims=True)

    def to_col(v):
        return jnp.sum(jnp.where(lan == sub, v, 0.0), axis=1, keepdims=True)

    stat = jnp.concatenate(
        [a_recv[k, n_rows : n_rows + 16, :].astype(F32)[0:1] for k in range(N_P)], axis=0
    )
    totals = pltpu.roll(stat, 128 - n_rows, 1) + pltpu.roll(stat, 128 - 2 * n_rows, 1)
    f_scores = [to_row(f.reshape(n_rows, 1)) for f in f_scores]
    top = jnp.maximum(jnp.max(stat, axis=0, keepdims=True), jnp.maximum(f_scores[0], f_scores[1]))
    used = lan[0:1] < n_rows
    w_dev = jnp.exp(jnp.where(used, stat - top, NEG))
    w_new = [jnp.exp(jnp.where(used, f - top, NEG)) for f in f_scores]
    denom = jnp.sum(w_dev * totals, axis=0, keepdims=True) + w_new[0] + w_new[1]
    denom = 1.0 / jnp.where(used, denom, 1.0)
    w_dev = w_dev * denom
    numer = jnp.zeros((n_rows, HD), F32)
    for n in range(2):
        vals = jnp.broadcast_to(f_s[n, 1][None], (OWN, TOK, HD)).reshape(n_rows, HD)
        numer = numer + to_col(w_new[n] * denom) * vals
    for k in range(N_P):
        numer = numer + to_col(w_dev[k : k + 1]) * a_recv[k, 0:n_rows, :].astype(F32)
    attention = numer.reshape(OWN, TOK, HD)
    attention = jnp.concatenate([attention[i] for i in range(OWN)], axis=1).astype(BF16)

    for cp in rt_cp:
        cp.wait_recv()
    rt_cp = [send(rt.at[core, x], rt.at[core, x], at_x(k)) for k in range(1, NX)]

    def packed(v):
        half = v.shape[1] // 2
        return jnp.concatenate([v[:, 0:half], v[:, half:]], axis=0)

    def unpacked(v):
        return jnp.concatenate([v[0:TOK], v[TOK : 2 * TOK]], axis=1)

    res_cp.wait()
    at = pl.ds(pl.multiple_of(y * PAIR, PAIR), PAIR)
    for s in range(2):
        r_s[pl.ds(REQS * s, REQS), :] = res_v[s, :, at].astype(F32)
    ow_cp.wait()
    b_cp = []
    for k in (2, 1, 3, 0):
        yy = lax.rem(y + k, NY)
        term = jnp.dot(
            attention,
            ow_v[:, pl.ds(pl.multiple_of(yy * PAIR, PAIR), PAIR)],
            preferred_element_type=F32,
        )
        if k != 0:
            b_send[k] = packed(term).astype(BF16)
            b_cp.append(send(b_send.at[k], b_recv.at[k], at_y(k)))
    hidden = packed(jnp.where(zhi == 0, r_s[...], 0.0) + term)
    for k, cp in zip((2, 1, 3), b_cp):
        cp.wait_recv()
        hidden = hidden + b_recv[k].astype(F32)
    zr[0] = hidden.astype(BF16)

    z_cp = {k: send(zr.at[0], zr.at[k], at_z(k)) for k in Z_LABELS}
    for cp in rt_cp:
        cp.wait_recv()
    rt_cp = [send(rt.at[core], rt.at[core], sibling)]
    b_cp, a_cp = [], []

    def to_ring(hh, jb):
        piece = g_buf.at[hh, core, ia, jb]
        return [send(piece, piece, at_a(k)) for k in (2, 1, 3)]

    for hh in range(2):
        for n, o in enumerate(OFFSETS[hh]):
            if o != 0:
                z_cp[o].wait_recv()
            z_cp[(o + 4) % 8].wait_recv()
            hidden = zr[o].astype(F32) + zr[(o + 4) % 8].astype(F32)
            g_buf[hh, core, ia, ib, n] = hidden.astype(BF16)
        mine = g_buf.at[hh, core, ia, ib]
        b_cp.append({k: send(mine, mine, at_b(k)) for k in (2, 1, 3)})
    hid[0] = hidden[0:TOK]
    hid[1] = hidden[TOK : 2 * TOK]
    for hh in range(2):
        a_cp.append([to_ring(hh, ib)])
    gain_cp.wait()
    ssq[...] = jnp.zeros_like(ssq)
    for hh in range(2):
        for k in (1, 3, 2):
            b_cp[hh][k].wait_recv()
            a_cp[hh].append(to_ring(hh, lax.rem(ib + 4 - k, 4)))

    def prepare(hh, plane, jb):
        def step(ja, _):
            xx = (1 - plane) * ja + plane * jb
            yy = plane * ja + (1 - plane) * jb
            blocks = g_buf[hh, plane, ja, jb].astype(F32)
            rows = jnp.concatenate(
                [
                    blocks[:, 0:TOK].reshape(2 * TOK, PART),
                    blocks[:, TOK : 2 * TOK].reshape(2 * TOK, PART),
                ],
                axis=1,
            )
            sq = rows * rows
            while sq.shape[1] > 128:
                half = sq.shape[1] // 2
                sq = sq[:, 0:half] + sq[:, half:]
            at_row = pl.ds(
                pl.multiple_of((hh * 2 + plane) * (ALL // 4) + xx * (2 * TOK), 2 * TOK), 2 * TOK
            )
            at_col = pl.ds(pl.multiple_of(yy * PAIR, PAIR), PAIR)
            ssq[at_row, :] += sq
            rows_v[at_row, at_col] = (rows * gain_v[:, at_col]).astype(BF16)
            return 0

        lax.fori_loop(0, 4, step, 0)

    def receive(hh):
        order = (0, 1, 3, 2)

        def across(ja, jb):
            piece = g_buf.at[hh, core, ja, jb]
            return send(piece, piece, sibling)

        c_cp = [[across(ia, lax.rem(ib + 4 - k, 4))] for k in order]
        for i, k in enumerate(order):
            jb = lax.rem(ib + 4 - k, 4)
            for ka, cp in zip((2, 1, 3), a_cp[hh][i]):
                cp.wait_recv()
                c_cp[i].append(across(lax.rem(ia + 4 - ka, 4), jb))
            prepare(hh, core, jb)
            if i > 0:
                for cp in c_cp[i - 1]:
                    cp.wait_recv()
                prepare(hh, 1 - core, lax.rem(sib_ib + 4 - order[i - 1], 4))
        for cp in c_cp[3]:
            cp.wait_recv()
        prepare(hh, 1 - core, lax.rem(sib_ib + 4 - order[3], 4))

    def experts(hh):
        here = slice(hh * (ALL // 2), (hh + 1) * (ALL // 2))
        spread = jnp.sum(ssq[here, :], -1, keepdims=True) * (1.0 / D)
        norm = lax.rsqrt(spread + 1e-06)
        coefs = rt[:, :, 2 * hh : 2 * hh + 2].reshape(ALL // 2, 128)
        lane = lax.broadcasted_iota(jnp.int32, (ALL // 2, 128), 1)
        for j in range(2):
            coef = jnp.sum(jnp.where(lane == 2 * me + j, coefs, 0.0), -1, keepdims=True)
            both = jnp.dot(
                rows_v[here, :], wgu_v[:, 256 * j : 256 * j + 256], preferred_element_type=F32
            )
            gate = both[:, 0:128] * norm
            up = both[:, 128:256] * norm
            inner = gate / (1.0 + jnp.exp(-gate)) * up
            act[here, 128 * j : 128 * j + 128] = (inner * coef).astype(BF16)

        def down_step(yy, _):
            at = pl.ds(pl.multiple_of(yy * PAIR, PAIR), PAIR)
            made = jnp.dot(act[here, :], wd_v[:, at], preferred_element_type=F32)
            made = made.reshape(2, NX * 2, TOK, PAIR)
            made = jnp.concatenate([made[..., 0:PART], made[..., PART:PAIR]], axis=2)
            made = made.astype(BF16).reshape(2, NX, 2, 2 * TOK, PART)
            p_buf[hh, 0, :, yy] = made[0]
            p_buf[hh, 1, yy] = made[1]
            return 0

        lax.fori_loop(0, NY, down_step, 0)

    order = (2, 1, 3, 0)

    def core_sends(hh):
        cps = []
        for kb in order:
            for ka in order:
                piece = (lax.rem(sib_ia + ka, 4), lax.rem(sib_ib + kb, 4))
                cps.append(send(p_buf.at[hh, 1 - core, *piece], s_buf.at[hh, *piece], sibling))
        return cps

    def ring_sends(hh, c_cp):
        cps = []
        for i, kb in enumerate(order):
            jb = lax.rem(ib + kb, 4)
            for n, ka in enumerate(order):
                ja = lax.rem(ia + ka, 4)
                c_cp[4 * i + n].wait_recv()
                both = p_buf[hh, core, ja, jb].astype(F32) + s_buf[hh, ja, jb].astype(F32)
                if ka != 0:
                    m_buf[hh, ja, jb] = both.astype(BF16)
                    cps.append(send(m_buf.at[hh, ja, jb], a_in.at[hh, i, ka], at_a(ka)))
                else:
                    n_buf[hh, i] = both
        return cps

    e_cp = []

    def last_sends(hh, ring_cp):
        for i, kb in enumerate(order):
            total = n_buf[hh, i]
            for n in range(3):
                ring_cp[3 * i + n].wait_recv()
                total = total + a_in[hh, i, order[n]].astype(F32)
            for n, o in enumerate(OFFSETS[hh]):
                t_buf[hh, i, n, 0] = total[n, 0:TOK]
                t_buf[hh, i, n, 1] = total[n, TOK : 2 * TOK]
                for kz in ((8 - o) % 8, 4 - o):
                    zz = lax.div(lax.rem(z + kz, N_Z), NZL)
                    if kb != 0 or kz != 0:
                        e_send[i, kz] = packed(t_buf[hh, i, n, zz]).astype(BF16)
                        cp = send(e_send.at[i, kz], e_recv.at[i, kz], at_bz(kb, kz))
                        e_cp.append((i, kz, cp))

    for cp in w_cp:
        cp.wait()
    for cp in wd_cp:
        cp.wait()
    receive(0)
    for cp in rt_cp:
        cp.wait_recv()
    experts(0)
    c_0 = core_sends(0)
    receive(1)
    a_0 = ring_sends(0, c_0)
    experts(1)
    c_1 = core_sends(1)
    a_1 = ring_sends(1, c_1)
    last_sends(0, a_0)
    last_sends(1, a_1)
    result = packed(hid[zhi]) + packed(t_buf[1, 3, 1, zhi])
    for i, kz, cp in e_cp:
        cp.wait_recv()
        result = result + e_recv[i, kz].astype(F32)
    o_s[...] = unpacked(result)
    for s in range(2):
        out_ref[s] = o_s[REQS * s : REQS * (s + 1), :].astype(BF16)
    guest_cp.wait_recv()
    for cp in sent:
        cp.wait_send()


def shards(
    queries,
    fresh_entries,
    cache_blocks,
    lengths,
    migration,
    residual,
    out_weight,
    norm_gain,
    routes,
    route_gates,
    w_gate,
    w_up,
    w_down,
):
    vmem = pl.BlockSpec(memory_space=pltpu.VMEM)
    hbm = pl.BlockSpec(memory_space=pltpu.HBM)
    pair = (2 * TOK, PART)
    block = (2 * TOK, HALF)

    def buf(*shape, dtype=BF16):
        return pltpu.VMEM(shape, dtype)

    shapes = (
        jax.ShapeDtypeStruct((2, REQS, PART), BF16),
        jax.ShapeDtypeStruct((8, ROWS, 512), BF16),
    )
    return pl.pallas_call(
        kernel,
        out_shape=tuple(pltpu.VMEM(v.shape, v.dtype) for v in shapes),
        in_specs=[hbm] * 13,
        out_specs=(vmem, vmem),
        scratch_shapes=[
            buf(2, REQS, D),
            buf(2, REQS, 512),
            buf(1, REQS, dtype=jnp.int32),
            pltpu.SMEM((2, 8), jnp.int32),
            buf(2, REQS, D),
            buf(1, D, dtype=F32),
            buf(2, REQS, TOPK, dtype=jnp.int32),
            buf(2, REQS, TOPK, dtype=F32),
            buf(REQS, BLOCKS, ROWS, 512),
            buf(PART, D),
            buf(D, 512),
            buf(256, D),
            buf(8, ROWS, 512),
            buf(TOK, D, dtype=F32),
            buf(QH * TOK, HD),
            buf(2, 2, TOK, HD, dtype=F32),
            buf(TOK, PAIR, dtype=F32),
            buf(N_P, OWN * TOK + 16, HD),
            buf(N_P, OWN * TOK + 16, HD),
            buf(NY, *pair),
            buf(NY, *pair),
            buf(N_Z, *pair),
            buf(2, TOK, PART, dtype=F32),
            buf(2, NX, NZL, TOK, 128, dtype=F32),
            buf(2, 2, 4, 4, 2, *pair),
            buf(ALL, D),
            buf(ALL, 128, dtype=F32),
            buf(ALL, 256),
            buf(2, 2, 4, 4, 2, *pair),
            buf(2, 4, 4, 2, *pair),
            buf(2, 4, 4, 2, *pair),
            buf(2, 4, 4, 2, *pair),
            buf(2, 4, 2, *pair, dtype=F32),
            buf(2, 4, 2, 2, TOK, PART, dtype=F32),
            buf(4, N_Z, *block),
            buf(4, N_Z, *block),
            buf(TOK, PART, dtype=F32),
            pltpu.SemaphoreType.DMA((24,)),
            pltpu.SemaphoreType.DMA((N_SEMS,)),
            pltpu.SemaphoreType.DMA((N_SEMS,)),
        ],
        compiler_params=pltpu.CompilerParams(
            collective_id=0, has_side_effects=True, vmem_limit_bytes=60 * MIB
        ),
        cost_estimate=pl.CostEstimate(
            flops=2_000_000_000, bytes_accessed=13 * MIB, transcendentals=200_000
        ),
    )(
        queries,
        fresh_entries,
        cache_blocks,
        lengths.reshape(1, REQS),
        migration.T,
        residual,
        out_weight,
        norm_gain.reshape(1, D),
        routes,
        route_gates,
        w_gate,
        w_up,
        w_down,
    )


def solution(mesh):
    in_specs = (
        P(None, "dp", None),
        P(None, "dp", None),
        P("dp", None, "expert", None),
        P("dp"),
        P("dp", None),
        P(None, "dp", None),
        P("expert", None),
        P(),
        P(None, "dp", None),
        P(None, "dp", None),
        P("dp", None, "expert"),
        P("dp", None, "expert"),
        P("dp", "expert", None),
    )
    out_specs = (P(None, "dp", "expert"), P("dp", "expert", None))
    return jax.shard_map(shards, mesh=mesh, in_specs=in_specs, out_specs=out_specs, check_vma=False)
```

```python
import functools
import math

import jax
import jax.numpy as jnp
from jax import lax
from jax.experimental import pallas as pl
from jax.experimental.pallas import tpu as pltpu
from jax.sharding import PartitionSpec as P

MESH = pl.DeviceIdType.MESH
HD = 128
QH = 32
KVH = 2
TOPK = 8
BLOCKS = 32
NX, NZL, NY, NZH = 4, 4, 4, 2
N_P = NY * NZH
N_Z = NZH * NZL
N_DP = NX * NZL * 2
REQS = 4
TOK = 2 * REQS
D = 4096
PART = D // N_P
HALF = PART // 2
PAIR = 2 * PART
Z_LABELS = (5, 6, 2, 1, 4, 3, 7)
OFFSETS = ((2, 1), (3, 0))
SLOT = {2: 0, 1: 1, 3: 2, 0: 3}
FAR_P = (3, 5, 1, 7, 4, 2, 6)
ROWS = 16
POSN = BLOCKS * ROWS
OWN = QH // N_P
ALL = N_DP * TOK
F32 = jnp.float32
BF16 = jnp.bfloat16
NEG = -1e30
N_SEMS = 180
MIB = 1024 * 1024


def kernel(
    q_ref,
    fresh_ref,
    cache_ref,
    len_ref,
    mig_ref,
    res_ref,
    ow_ref,
    gain_ref,
    routes_ref,
    gates_ref,
    wg_ref,
    wu_ref,
    wd_ref,
    out_ref,
    guest_ref,
    q_v,
    fresh_v,
    len_v,
    mig_s,
    res_v,
    gain_v,
    routes_v,
    gates_v,
    cache_v,
    ow_v,
    wgu_v,
    wd_v,
    picked_v,
    q_s,
    q_b,
    f_s,
    r_s,
    a_send,
    a_recv,
    b_send,
    b_recv,
    zr,
    hid,
    rt,
    g_buf,
    rows_v,
    ssq,
    act,
    p_buf,
    s_buf,
    m_buf,
    a_in,
    n_buf,
    t_buf,
    e_send,
    e_recv,
    o_s,
    load_sem,
    send_sem,
    recv_sem,
):
    me = lax.axis_index("dp")
    p = lax.axis_index("expert")
    core = lax.rem(me, 2)
    zlo = lax.rem(lax.div(me, 2), NZL)
    x = lax.div(me, 2 * NZL)
    y = lax.div(p, NZH)
    zhi = lax.rem(p, NZH)
    z = zhi * NZL + zlo

    def place(x_, y_, zlo_, zhi_, core_):
        return ((x_ * NZL + zlo_) * 2 + core_, y_ * NZH + zhi_)

    def at_p(k):
        return (me, lax.rem(p + k, N_P))

    def at_y(k):
        return place(x, lax.rem(y + k, NY), zlo, zhi, core)

    def at_z(k):
        t = lax.rem(z + k, N_Z)
        return place(x, y, lax.rem(t, NZL), lax.div(t, NZL), core)

    def at_x(k):
        return place(lax.rem(x + k, NX), y, zlo, zhi, core)

    def at_zlo(k):
        return place(x, y, lax.rem(zlo + k, NZL), zhi, core)

    def at_a(k):
        return place(lax.rem(x + (1 - core) * k, NX), lax.rem(y + core * k, NY), zlo, zhi, core)

    def at_b(k):
        return place(lax.rem(x + core * k, NX), lax.rem(y + (1 - core) * k, NY), zlo, zhi, core)

    def at_bz(kb, kz):
        t = lax.rem(z + kz, N_Z)
        return place(
            lax.rem(x + core * kb, NX),
            lax.rem(y + (1 - core) * kb, NY),
            lax.rem(t, NZL),
            lax.div(t, NZL),
            core,
        )

    sibling = place(x, y, zlo, zhi, 1 - core)
    ia = (1 - core) * x + core * y
    ib = core * x + (1 - core) * y
    sib_ib = ia
    sib_ia = ib

    barrier = pltpu.get_barrier_semaphore()
    peers = [at_p(k) for k in range(1, N_P)]
    peers += [at_z(k) for k in range(1, N_Z) if k != NZL]
    peers += [at_x(k) for k in range(1, NX)]
    peers += [at_bz(kb, kz) for kb in range(1, 4) for kz in range(1, N_Z)]
    peers += [sibling]
    for peer in peers:
        pl.semaphore_signal(barrier, inc=1, device_id=peer, device_id_type=MESH)

    loads = []

    def load(src, dst):
        cp = pltpu.make_async_copy(src, dst, load_sem.at[len(loads)])
        cp.start()
        loads.append(cp)
        return cp

    small_cp = [load(routes_ref, routes_v), load(gates_ref, gates_v), load(q_ref, q_v)]
    len_cp = load(len_ref, len_v)
    mig_cp = load(mig_ref, mig_s)
    cache_cp = [load(cache_ref.at[r], cache_v.at[r]) for r in range(REQS)]
    fresh_cp = load(fresh_ref, fresh_v)
    res_cp = load(res_ref, res_v)
    gain_cp = load(gain_ref, gain_v)
    sent = []

    def send(src, dst, peer):
        k = len(sent)
        cp = pltpu.make_async_remote_copy(
            src_ref=src,
            dst_ref=dst,
            send_sem=send_sem.at[k],
            recv_sem=recv_sem.at[k],
            device_id=peer,
            device_id_type=MESH,
        )
        cp.start()
        sent.append(cp)
        return cp

    for cp in small_cp:
        cp.wait()

    lane = lax.broadcasted_iota(jnp.int32, (REQS, 128), 1)
    for s in range(2):
        ids = routes_v[s]
        vals = gates_v[s]
        coef = jnp.zeros((REQS, 128), F32)
        for k in range(TOPK):
            coef = coef + jnp.where(lane == ids[:, k : k + 1], vals[:, k : k + 1], 0.0)
        rt[core, x, SLOT[0], pl.ds(REQS * s, REQS), :] = coef

    for s in range(2):
        q_s[pl.ds(REQS * s, REQS), :] = q_v[s].astype(F32)
    q_b[...] = jnp.concatenate(
        [q_s[:, h * HD : (h + 1) * HD] for h in range(QH)], axis=0
    ).astype(BF16)

    mig_cp.wait()
    len_cp.wait()
    for cp in cache_cp:
        cp.wait()
    ow_cp = load(ow_ref, ow_v)
    w_cp = []
    for j in range(2):
        w_cp.append(load(wg_ref.at[j], wgu_v.at[:, pl.ds(256 * j, 128)]))
        w_cp.append(load(wu_ref.at[j], wgu_v.at[:, pl.ds(256 * j + 128, 128)]))
    wd_cp = [load(wd_ref.at[j], wd_v.at[pl.ds(128 * j, 128)]) for j in range(2)]
    for m in range(8):
        picked_v[m] = cache_v[mig_s[0, m], mig_s[1, m]]

    scale = 1.0 / math.sqrt(HD)
    col = lax.broadcasted_iota(jnp.int32, (TOK, POSN), 1)
    row = lax.rem(lax.broadcasted_iota(jnp.int32, (TOK, POSN), 0), REQS)
    position = lax.div(col, ROWS) * (ROWS * N_P) + p * ROWS + lax.rem(col, ROWS)
    limit = jnp.full((TOK, POSN), 0, jnp.int32)
    for r in range(REQS):
        limit = jnp.where(row == r, len_v[0:1, r : r + 1], limit)
    valid = position < limit
    hk = QH // KVH * TOK
    rid = lax.rem(lax.broadcasted_iota(jnp.int32, (hk, POSN), 0), REQS)
    rid_o = lax.rem(lax.broadcasted_iota(jnp.int32, (hk, HD), 0), REQS)
    sub = lax.broadcasted_iota(jnp.int32, (OWN * TOK, 128), 0)
    lan = lax.broadcasted_iota(jnp.int32, (OWN * TOK, 128), 1)
    for k in range(KVH):
        qk = q_b[k * hk : (k + 1) * hk]
        scores = None
        for r in range(REQS):
            keys = cache_v[r, :, :, k * HD : (k + 1) * HD].reshape(POSN, HD)
            part = lax.dot_general(
                qk, keys, (((1,), (1,)), ((), ())), preferred_element_type=F32
            )
            scores = part if r == 0 else jnp.where(rid == r, part, scores)
        scores = scores.reshape(hk // TOK, TOK, POSN)
        scores = jnp.where(valid[None], scores * scale, NEG)
        peak = jnp.max(scores, -1, keepdims=True).astype(BF16).astype(F32)
        weights = jnp.exp(scores - peak)
        total = jnp.sum(weights, -1, keepdims=True)
        weights = weights.reshape(hk, POSN).astype(BF16)
        state = None
        for r in range(REQS):
            vals = cache_v[r, :, :, (KVH + k) * HD : (KVH + k + 1) * HD].reshape(POSN, HD)
            part = jnp.dot(weights, vals, preferred_element_type=F32)
            state = part if r == 0 else jnp.where(rid_o == r, part, state)
        peak = peak.reshape(hk, 1)
        total = total.reshape(hk, 1)
        total_hi = total.astype(BF16).astype(F32)
        total_lo = total - total_hi
        n_rows = OWN * TOK
        for i in range(hk // n_rows):
            dest = k * (hk // n_rows) + i
            rows = slice(i * n_rows, (i + 1) * n_rows)
            a_send[dest, 0:n_rows, :] = state[rows].astype(BF16)
            stat = jnp.where(lan == sub, peak[rows], 0.0)
            stat = jnp.where(lan == sub + n_rows, total_hi[rows], stat)
            stat = jnp.where(lan == sub + 2 * n_rows, total_lo[rows], stat)
            stat = jnp.sum(stat, axis=0, keepdims=True)
            a_send[dest, n_rows : n_rows + 16, :] = jnp.broadcast_to(stat, (16, 128)).astype(BF16)

    pl.semaphore_wait(barrier, len(peers))

    a_cp = []
    for k in FAR_P:
        a_cp.append(send(a_send.at[lax.rem(p + k, N_P)], a_recv.at[k], at_p(k)))
    rt_cp = [
        send(rt.at[core, x, SLOT[0]], rt.at[core, x, SLOT[k]], at_zlo(k))
        for k in range(1, NZL)
    ]
    guest_cp = send(picked_v, guest_ref, at_x(2))
    a_recv[0] = a_send[p]

    fresh_cp.wait()
    kv = lax.div(p, N_P // KVH)
    for n in range(2):
        for j in range(2):
            new = fresh_v[
                n, :, pl.ds(pl.multiple_of((j * KVH + kv) * HD, HD), HD)
            ].astype(F32)
            f_s[n, j, 0:REQS, :] = new
            f_s[n, j, REQS:TOK, :] = new
    q_own = q_s[:, pl.ds(pl.multiple_of(p * PART, PART), PART)]
    q_own = jnp.stack([q_own[:, i * HD : (i + 1) * HD] for i in range(OWN)], axis=0)
    f_scores = [
        jnp.sum(q_own * f_s[n, 0][None], -1, keepdims=True) * scale for n in range(2)
    ]
    step_row = lax.broadcasted_iota(jnp.int32, (OWN, TOK, 1), 1)
    f_scores[1] = jnp.where(step_row >= REQS, f_scores[1], NEG)

    for cp in a_cp:
        cp.wait_recv()
    n_rows = OWN * TOK

    def to_row(v):
        return jnp.sum(jnp.where(lan == sub, v, 0.0), axis=0, keepdims=True)

    def to_col(v):
        return jnp.sum(jnp.where(lan == sub, v, 0.0), axis=1, keepdims=True)

    stat = jnp.concatenate(
        [a_recv[k, n_rows : n_rows + 16, :].astype(F32)[0:1] for k in range(N_P)], axis=0
    )
    totals = pltpu.roll(stat, 128 - n_rows, 1) + pltpu.roll(stat, 128 - 2 * n_rows, 1)
    f_scores = [to_row(f.reshape(n_rows, 1)) for f in f_scores]
    top = jnp.maximum(jnp.max(stat, axis=0, keepdims=True), jnp.maximum(f_scores[0], f_scores[1]))
    used = lan[0:1] < n_rows
    w_dev = jnp.exp(jnp.where(used, stat - top, NEG))
    w_new = [jnp.exp(jnp.where(used, f - top, NEG)) for f in f_scores]
    denom = jnp.sum(w_dev * totals, axis=0, keepdims=True) + w_new[0] + w_new[1]
    denom = 1.0 / jnp.where(used, denom, 1.0)
    w_dev = w_dev * denom
    numer = jnp.zeros((n_rows, HD), F32)
    for n in range(2):
        vals = jnp.broadcast_to(f_s[n, 1][None], (OWN, TOK, HD)).reshape(n_rows, HD)
        numer = numer + to_col(w_new[n] * denom) * vals
    for k in range(N_P):
        numer = numer + to_col(w_dev[k : k + 1]) * a_recv[k, 0:n_rows, :].astype(F32)
    attention = numer.reshape(OWN, TOK, HD)
    attention = jnp.concatenate([attention[i] for i in range(OWN)], axis=1).astype(BF16)

    for cp in rt_cp:
        cp.wait_recv()
    rt_cp = [send(rt.at[core, x], rt.at[core, x], at_x(k)) for k in range(1, NX)]

    def packed(v):
        half = v.shape[1] // 2
        return jnp.concatenate([v[:, 0:half], v[:, half:]], axis=0)

    def unpacked(v):
        return jnp.concatenate([v[0:TOK], v[TOK : 2 * TOK]], axis=1)

    res_cp.wait()
    at = pl.ds(pl.multiple_of(y * PAIR, PAIR), PAIR)
    for s in range(2):
        r_s[pl.ds(REQS * s, REQS), :] = res_v[s, :, at].astype(F32)
    ow_cp.wait()
    b_cp = []
    for k in (2, 1, 3, 0):
        yy = lax.rem(y + k, NY)
        term = jnp.dot(
            attention,
            ow_v[:, pl.ds(pl.multiple_of(yy * PAIR, PAIR), PAIR)],
            preferred_element_type=F32,
        )
        if k != 0:
            b_send[k] = packed(term).astype(BF16)
            b_cp.append(send(b_send.at[k], b_recv.at[k], at_y(k)))
    hidden = packed(jnp.where(zhi == 0, r_s[...], 0.0) + term)
    for k, cp in zip((2, 1, 3), b_cp):
        cp.wait_recv()
        hidden = hidden + b_recv[k].astype(F32)
    zr[0] = hidden.astype(BF16)

    z_cp = {k: send(zr.at[0], zr.at[k], at_z(k)) for k in Z_LABELS}
    for cp in rt_cp:
        cp.wait_recv()
    rt_cp = [send(rt.at[core], rt.at[core], sibling)]
    b_cp, a_cp = [], []

    def to_ring(hh, jb):
        piece = g_buf.at[hh, core, ia, jb]
        return [send(piece, piece, at_a(k)) for k in (2, 1, 3)]

    for hh in range(2):
        for n, o in enumerate(OFFSETS[hh]):
            if o != 0:
                z_cp[o].wait_recv()
            z_cp[(o + 4) % 8].wait_recv()
            hidden = zr[o].astype(F32) + zr[(o + 4) % 8].astype(F32)
            g_buf[hh, core, ia, ib, n] = hidden.astype(BF16)
        mine = g_buf.at[hh, core, ia, ib]
        b_cp.append({k: send(mine, mine, at_b(k)) for k in (2, 1, 3)})
    hid[0] = hidden[0:TOK]
    hid[1] = hidden[TOK : 2 * TOK]
    for hh in range(2):
        a_cp.append([to_ring(hh, ib)])
    gain_cp.wait()
    ssq[...] = jnp.zeros_like(ssq)
    for hh in range(2):
        for k in (1, 3, 2):
            b_cp[hh][k].wait_recv()
            a_cp[hh].append(to_ring(hh, lax.rem(ib + 4 - k, 4)))

    def prepare(hh, plane, jb):
        def step(ja, _):
            xx = (1 - plane) * ja + plane * jb
            yy = plane * ja + (1 - plane) * jb
            blocks = g_buf[hh, plane, ja, jb].astype(F32)
            rows = jnp.concatenate(
                [
                    blocks[:, 0:TOK].reshape(2 * TOK, PART),
                    blocks[:, TOK : 2 * TOK].reshape(2 * TOK, PART),
                ],
                axis=1,
            )
            sq = rows * rows
            while sq.shape[1] > 128:
                half = sq.shape[1] // 2
                sq = sq[:, 0:half] + sq[:, half:]
            at_row = pl.ds(
                pl.multiple_of((hh * 2 + plane) * (ALL // 4) + xx * (2 * TOK), 2 * TOK), 2 * TOK
            )
            at_col = pl.ds(pl.multiple_of(yy * PAIR, PAIR), PAIR)
            ssq[at_row, :] += sq
            rows_v[at_row, at_col] = (rows * gain_v[:, at_col]).astype(BF16)
            return 0

        for ja in range(4):
            step(ja, 0)

    def receive(hh):
        order = (0, 1, 3, 2)

        def across(ja, jb):
            piece = g_buf.at[hh, core, ja, jb]
            return send(piece, piece, sibling)

        c_cp = [[across(ia, lax.rem(ib + 4 - k, 4))] for k in order]
        for i, k in enumerate(order):
            jb = lax.rem(ib + 4 - k, 4)
            for ka, cp in zip((2, 1, 3), a_cp[hh][i]):
                cp.wait_recv()
                c_cp[i].append(across(lax.rem(ia + 4 - ka, 4), jb))
            prepare(hh, core, jb)
            if i > 0:
                for cp in c_cp[i - 1]:
                    cp.wait_recv()
                prepare(hh, 1 - core, lax.rem(sib_ib + 4 - order[i - 1], 4))
        for cp in c_cp[3]:
            cp.wait_recv()
        prepare(hh, 1 - core, lax.rem(sib_ib + 4 - order[3], 4))

    def experts(hh):
        here = slice(hh * (ALL // 2), (hh + 1) * (ALL // 2))
        spread = jnp.sum(ssq[here, :], -1, keepdims=True) * (1.0 / D)
        norm = lax.rsqrt(spread + 1e-06)
        coefs = rt[:, :, 2 * hh : 2 * hh + 2].reshape(ALL // 2, 128)
        lane = lax.broadcasted_iota(jnp.int32, (ALL // 2, 128), 1)
        all_up = jnp.dot(rows_v[here, :], wgu_v[...], preferred_element_type=F32)
        for j in range(2):
            coef = jnp.sum(jnp.where(lane == 2 * me + j, coefs, 0.0), -1, keepdims=True)
            both = all_up[:, 256 * j : 256 * j + 256]
            gate = both[:, 0:128] * norm
            up = both[:, 128:256] * norm
            inner = gate / (1.0 + jnp.exp(-gate)) * up
            act[here, 128 * j : 128 * j + 128] = (inner * coef).astype(BF16)

        def down_step(yy, _):
            at = pl.ds(pl.multiple_of(yy * PAIR, PAIR), PAIR)
            made = jnp.dot(act[here, :], wd_v[:, at], preferred_element_type=F32)
            made = made.reshape(2, NX * 2, TOK, PAIR)
            made = jnp.concatenate([made[..., 0:PART], made[..., PART:PAIR]], axis=2)
            made = made.astype(BF16).reshape(2, NX, 2, 2 * TOK, PART)
            p_buf[hh, 0, :, yy] = made[0]
            p_buf[hh, 1, yy] = made[1]
            return 0

        for k in range(NY):
            down_step(k, 0)

    order = (2, 1, 3, 0)

    def core_sends(hh):
        cps = []
        for kb in order:
            for ka in order:
                piece = (lax.rem(sib_ia + ka, 4), lax.rem(sib_ib + kb, 4))
                cps.append(send(p_buf.at[hh, 1 - core, *piece], s_buf.at[hh, *piece], sibling))
        return cps

    def ring_sends(hh, c_cp):
        cps = []
        for i, kb in enumerate(order):
            jb = lax.rem(ib + kb, 4)
            for n, ka in enumerate(order):
                ja = lax.rem(ia + ka, 4)
                c_cp[4 * i + n].wait_recv()
                both = p_buf[hh, core, ja, jb].astype(F32) + s_buf[hh, ja, jb].astype(F32)
                if ka != 0:
                    m_buf[hh, ja, jb] = both.astype(BF16)
                    cps.append(send(m_buf.at[hh, ja, jb], a_in.at[hh, i, ka], at_a(ka)))
                else:
                    n_buf[hh, i] = both
        return cps

    e_cp = []

    def last_sends(hh, ring_cp):
        for i, kb in enumerate(order):
            total = n_buf[hh, i]
            for n in range(3):
                ring_cp[3 * i + n].wait_recv()
                total = total + a_in[hh, i, order[n]].astype(F32)
            for n, o in enumerate(OFFSETS[hh]):
                t_buf[hh, i, n, 0] = total[n, 0:TOK]
                t_buf[hh, i, n, 1] = total[n, TOK : 2 * TOK]
                for kz in ((8 - o) % 8, 4 - o):
                    zz = lax.div(lax.rem(z + kz, N_Z), NZL)
                    if kb != 0 or kz != 0:
                        e_send[i, kz] = packed(t_buf[hh, i, n, zz]).astype(BF16)
                        cp = send(e_send.at[i, kz], e_recv.at[i, kz], at_bz(kb, kz))
                        e_cp.append((i, kz, cp))

    for cp in w_cp:
        cp.wait()
    for cp in wd_cp:
        cp.wait()
    receive(0)
    for cp in rt_cp:
        cp.wait_recv()
    experts(0)
    c_0 = core_sends(0)
    receive(1)
    a_0 = ring_sends(0, c_0)
    experts(1)
    c_1 = core_sends(1)
    guest_cp.wait_recv()
    a_1 = ring_sends(1, c_1)
    last_sends(0, a_0)
    last_sends(1, a_1)
    n_last = len(sent) - len(e_cp)
    for cp in sent[:n_last]:
        cp.wait_send()
    result = packed(hid[zhi]) + packed(t_buf[1, 3, 1, zhi])
    for i, kz, cp in e_cp:
        cp.wait_recv()
        result = result + e_recv[i, kz].astype(F32)
    o_s[...] = unpacked(result)
    for s in range(2):
        out_ref[s] = o_s[REQS * s : REQS * (s + 1), :].astype(BF16)
    for cp in sent[n_last:]:
        cp.wait_send()


def shards(
    queries,
    fresh_entries,
    cache_blocks,
    lengths,
    migration,
    residual,
    out_weight,
    norm_gain,
    routes,
    route_gates,
    w_gate,
    w_up,
    w_down,
):
    vmem = pl.BlockSpec(memory_space=pltpu.VMEM)
    hbm = pl.BlockSpec(memory_space=pltpu.HBM)
    pair = (2 * TOK, PART)
    block = (2 * TOK, HALF)

    def buf(*shape, dtype=BF16):
        return pltpu.VMEM(shape, dtype)

    shapes = (
        jax.ShapeDtypeStruct((2, REQS, PART), BF16),
        jax.ShapeDtypeStruct((8, ROWS, 512), BF16),
    )
    return pl.pallas_call(
        kernel,
        out_shape=tuple(pltpu.VMEM(v.shape, v.dtype) for v in shapes),
        in_specs=[hbm] * 13,
        out_specs=(vmem, vmem),
        scratch_shapes=[
            buf(2, REQS, D),
            buf(2, REQS, 512),
            buf(1, REQS, dtype=jnp.int32),
            pltpu.SMEM((2, 8), jnp.int32),
            buf(2, REQS, D),
            buf(1, D, dtype=F32),
            buf(2, REQS, TOPK, dtype=jnp.int32),
            buf(2, REQS, TOPK, dtype=F32),
            buf(REQS, BLOCKS, ROWS, 512),
            buf(PART, D),
            buf(D, 512),
            buf(256, D),
            buf(8, ROWS, 512),
            buf(TOK, D, dtype=F32),
            buf(QH * TOK, HD),
            buf(2, 2, TOK, HD, dtype=F32),
            buf(TOK, PAIR, dtype=F32),
            buf(N_P, OWN * TOK + 16, HD),
            buf(N_P, OWN * TOK + 16, HD),
            buf(NY, *pair),
            buf(NY, *pair),
            buf(N_Z, *pair),
            buf(2, TOK, PART, dtype=F32),
            buf(2, NX, NZL, TOK, 128, dtype=F32),
            buf(2, 2, 4, 4, 2, *pair),
            buf(ALL, D),
            buf(ALL, 128, dtype=F32),
            buf(ALL, 256),
            buf(2, 2, 4, 4, 2, *pair),
            buf(2, 4, 4, 2, *pair),
            buf(2, 4, 4, 2, *pair),
            buf(2, 4, 4, 2, *pair),
            buf(2, 4, 2, *pair, dtype=F32),
            buf(2, 4, 2, 2, TOK, PART, dtype=F32),
            buf(4, N_Z, *block),
            buf(4, N_Z, *block),
            buf(TOK, PART, dtype=F32),
            pltpu.SemaphoreType.DMA((24,)),
            pltpu.SemaphoreType.DMA((N_SEMS,)),
            pltpu.SemaphoreType.DMA((N_SEMS,)),
        ],
        compiler_params=pltpu.CompilerParams(
            collective_id=0, has_side_effects=True, vmem_limit_bytes=60 * MIB
        ),
        cost_estimate=pl.CostEstimate(
            flops=2_000_000_000, bytes_accessed=13 * MIB, transcendentals=200_000
        ),
    )(
        queries,
        fresh_entries,
        cache_blocks,
        lengths.reshape(1, REQS),
        migration.T,
        residual,
        out_weight,
        norm_gain.reshape(1, D),
        routes,
        route_gates,
        w_gate,
        w_up,
        w_down,
    )


def solution(mesh):
    in_specs = (
        P(None, "dp", None),
        P(None, "dp", None),
        P("dp", None, "expert", None),
        P("dp"),
        P("dp", None),
        P(None, "dp", None),
        P("expert", None),
        P(),
        P(None, "dp", None),
        P(None, "dp", None),
        P("dp", None, "expert"),
        P("dp", None, "expert"),
        P("dp", "expert", None),
    )
    out_specs = (P(None, "dp", "expert"), P("dp", "expert", None))
    return jax.shard_map(shards, mesh=mesh, in_specs=in_specs, out_specs=out_specs, check_vma=False)
```

```python
import functools
import math

import jax
import jax.numpy as jnp
from jax import lax
from jax.experimental import pallas as pl
from jax.experimental.pallas import tpu as pltpu
from jax.sharding import PartitionSpec as P

MESH = pl.DeviceIdType.MESH
HD = 128
QH = 32
KVH = 2
TOPK = 8
BLOCKS = 32
NX, NZL, NY, NZH = 4, 4, 4, 2
N_P = NY * NZH
N_Z = NZH * NZL
N_DP = NX * NZL * 2
REQS = 4
TOK = 2 * REQS
D = 4096
PART = D // N_P
HALF = PART // 2
PAIR = 2 * PART
Z_LABELS = (5, 6, 2, 1, 4, 3, 7)
OFFSETS = ((2, 1), (3, 0))
SLOT = {2: 0, 1: 1, 3: 2, 0: 3}
FAR_P = (3, 5, 1, 7, 4, 2, 6)
ROWS = 16
POSN = BLOCKS * ROWS
OWN = QH // N_P
ALL = N_DP * TOK
F32 = jnp.float32
BF16 = jnp.bfloat16
NEG = -1e30
N_SEMS = 180
MIB = 1024 * 1024


def kernel(
    q_ref,
    fresh_ref,
    cache_ref,
    len_ref,
    mig_ref,
    res_ref,
    ow_ref,
    gain_ref,
    routes_ref,
    gates_ref,
    wg_ref,
    wu_ref,
    wd_ref,
    out_ref,
    guest_ref,
    q_v,
    fresh_v,
    len_v,
    mig_s,
    res_v,
    gain_v,
    routes_v,
    gates_v,
    cache_v,
    ow_v,
    wgu_v,
    wd_v,
    picked_v,
    q_s,
    q_b,
    f_s,
    r_s,
    a_send,
    a_recv,
    b_send,
    b_recv,
    zr,
    hid,
    rt,
    g_buf,
    rows_v,
    ssq,
    act,
    p_buf,
    s_buf,
    m_buf,
    a_in,
    n_buf,
    t_buf,
    e_send,
    e_recv,
    o_s,
    load_sem,
    send_sem,
    recv_sem,
):
    me = lax.axis_index("dp")
    p = lax.axis_index("expert")
    core = lax.rem(me, 2)
    zlo = lax.rem(lax.div(me, 2), NZL)
    x = lax.div(me, 2 * NZL)
    y = lax.div(p, NZH)
    zhi = lax.rem(p, NZH)
    z = zhi * NZL + zlo

    def place(x_, y_, zlo_, zhi_, core_):
        return ((x_ * NZL + zlo_) * 2 + core_, y_ * NZH + zhi_)

    def at_p(k):
        return (me, lax.rem(p + k, N_P))

    def at_y(k):
        return place(x, lax.rem(y + k, NY), zlo, zhi, core)

    def at_z(k):
        t = lax.rem(z + k, N_Z)
        return place(x, y, lax.rem(t, NZL), lax.div(t, NZL), core)

    def at_x(k):
        return place(lax.rem(x + k, NX), y, zlo, zhi, core)

    def at_zlo(k):
        return place(x, y, lax.rem(zlo + k, NZL), zhi, core)

    def at_a(k):
        return place(lax.rem(x + (1 - core) * k, NX), lax.rem(y + core * k, NY), zlo, zhi, core)

    def at_b(k):
        return place(lax.rem(x + core * k, NX), lax.rem(y + (1 - core) * k, NY), zlo, zhi, core)

    def at_bz(kb, kz):
        t = lax.rem(z + kz, N_Z)
        return place(
            lax.rem(x + core * kb, NX),
            lax.rem(y + (1 - core) * kb, NY),
            lax.rem(t, NZL),
            lax.div(t, NZL),
            core,
        )

    sibling = place(x, y, zlo, zhi, 1 - core)
    ia = (1 - core) * x + core * y
    ib = core * x + (1 - core) * y
    sib_ib = ia
    sib_ia = ib

    barrier = pltpu.get_barrier_semaphore()
    peers = [at_p(k) for k in range(1, N_P)]
    peers += [at_z(k) for k in range(1, N_Z) if k != NZL]
    peers += [at_x(k) for k in range(1, NX)]
    peers += [at_bz(kb, kz) for kb in range(1, 4) for kz in range(1, N_Z)]
    peers += [sibling]
    for peer in peers:
        pl.semaphore_signal(barrier, inc=1, device_id=peer, device_id_type=MESH)

    loads = []

    def load(src, dst):
        cp = pltpu.make_async_copy(src, dst, load_sem.at[len(loads)])
        cp.start()
        loads.append(cp)
        return cp

    small_cp = [load(routes_ref, routes_v), load(gates_ref, gates_v), load(q_ref, q_v)]
    len_cp = load(len_ref, len_v)
    mig_cp = load(mig_ref, mig_s)
    cache_cp = [load(cache_ref.at[r], cache_v.at[r]) for r in range(REQS)]
    fresh_cp = load(fresh_ref, fresh_v)
    res_cp = load(res_ref, res_v)
    gain_cp = load(gain_ref, gain_v)
    sent = []

    def send(src, dst, peer):
        k = len(sent)
        cp = pltpu.make_async_remote_copy(
            src_ref=src,
            dst_ref=dst,
            send_sem=send_sem.at[k],
            recv_sem=recv_sem.at[k],
            device_id=peer,
            device_id_type=MESH,
        )
        cp.start()
        sent.append(cp)
        return cp

    for cp in small_cp:
        cp.wait()

    lane = lax.broadcasted_iota(jnp.int32, (REQS, 128), 1)
    for s in range(2):
        ids = routes_v[s]
        vals = gates_v[s]
        coef = jnp.zeros((REQS, 128), F32)
        for k in range(TOPK):
            coef = coef + jnp.where(lane == ids[:, k : k + 1], vals[:, k : k + 1], 0.0)
        rt[core, x, SLOT[0], pl.ds(REQS * s, REQS), :] = coef

    for s in range(2):
        q_s[pl.ds(REQS * s, REQS), :] = q_v[s].astype(F32)
    q_b[...] = jnp.concatenate(
        [q_s[:, h * HD : (h + 1) * HD] for h in range(QH)], axis=0
    ).astype(BF16)

    mig_cp.wait()
    len_cp.wait()
    for cp in cache_cp:
        cp.wait()
    ow_cp = load(ow_ref, ow_v)
    w_cp = []
    for j in range(2):
        w_cp.append(load(wg_ref.at[j], wgu_v.at[:, pl.ds(256 * j, 128)]))
        w_cp.append(load(wu_ref.at[j], wgu_v.at[:, pl.ds(256 * j + 128, 128)]))
    wd_cp = [load(wd_ref.at[j], wd_v.at[pl.ds(128 * j, 128)]) for j in range(2)]
    for m in range(8):
        picked_v[m] = cache_v[mig_s[0, m], mig_s[1, m]]

    scale = 1.0 / math.sqrt(HD)
    col = lax.broadcasted_iota(jnp.int32, (TOK, POSN), 1)
    row = lax.rem(lax.broadcasted_iota(jnp.int32, (TOK, POSN), 0), REQS)
    position = lax.div(col, ROWS) * (ROWS * N_P) + p * ROWS + lax.rem(col, ROWS)
    limit = jnp.full((TOK, POSN), 0, jnp.int32)
    for r in range(REQS):
        limit = jnp.where(row == r, len_v[0:1, r : r + 1], limit)
    valid = position < limit
    hk = QH // KVH * TOK
    rid = lax.rem(lax.broadcasted_iota(jnp.int32, (hk, POSN), 0), REQS)
    rid_o = lax.rem(lax.broadcasted_iota(jnp.int32, (hk, HD), 0), REQS)
    sub = lax.broadcasted_iota(jnp.int32, (OWN * TOK, 128), 0)
    lan = lax.broadcasted_iota(jnp.int32, (OWN * TOK, 128), 1)
    for k in range(KVH):
        qk = q_b[k * hk : (k + 1) * hk]
        scores = None
        for r in range(REQS):
            keys = cache_v[r, :, :, k * HD : (k + 1) * HD].reshape(POSN, HD)
            part = lax.dot_general(
                qk, keys, (((1,), (1,)), ((), ())), preferred_element_type=F32
            )
            scores = part if r == 0 else jnp.where(rid == r, part, scores)
        scores = scores.reshape(hk // TOK, TOK, POSN)
        scores = jnp.where(valid[None], scores * scale, NEG)
        peak = jnp.max(scores, -1, keepdims=True).astype(BF16).astype(F32)
        weights = jnp.exp(scores - peak)
        total = jnp.sum(weights, -1, keepdims=True)
        weights = weights.reshape(hk, POSN).astype(BF16)
        state = None
        for r in range(REQS):
            vals = cache_v[r, :, :, (KVH + k) * HD : (KVH + k + 1) * HD].reshape(POSN, HD)
            part = jnp.dot(weights, vals, preferred_element_type=F32)
            state = part if r == 0 else jnp.where(rid_o == r, part, state)
        peak = peak.reshape(hk, 1)
        total = total.reshape(hk, 1)
        total_hi = total.astype(BF16).astype(F32)
        total_lo = total - total_hi
        n_rows = OWN * TOK
        for i in range(hk // n_rows):
            dest = k * (hk // n_rows) + i
            rows = slice(i * n_rows, (i + 1) * n_rows)
            a_send[dest, 0:n_rows, :] = state[rows].astype(BF16)
            stat = jnp.where(lan == sub, peak[rows], 0.0)
            stat = jnp.where(lan == sub + n_rows, total_hi[rows], stat)
            stat = jnp.where(lan == sub + 2 * n_rows, total_lo[rows], stat)
            stat = jnp.sum(stat, axis=0, keepdims=True)
            a_send[dest, n_rows : n_rows + 16, :] = jnp.broadcast_to(stat, (16, 128)).astype(BF16)

    pl.semaphore_wait(barrier, len(peers))

    a_cp = []
    for k in FAR_P:
        a_cp.append(send(a_send.at[lax.rem(p + k, N_P)], a_recv.at[k], at_p(k)))
    rt_cp = [
        send(rt.at[core, x, SLOT[0]], rt.at[core, x, SLOT[k]], at_zlo(k))
        for k in range(1, NZL)
    ]
    guest_cp = send(picked_v, guest_ref, at_x(2))
    a_recv[0] = a_send[p]

    fresh_cp.wait()
    kv = lax.div(p, N_P // KVH)
    for n in range(2):
        for j in range(2):
            new = fresh_v[
                n, :, pl.ds(pl.multiple_of((j * KVH + kv) * HD, HD), HD)
            ].astype(F32)
            f_s[n, j, 0:REQS, :] = new
            f_s[n, j, REQS:TOK, :] = new
    q_own = q_s[:, pl.ds(pl.multiple_of(p * PART, PART), PART)]
    q_own = jnp.stack([q_own[:, i * HD : (i + 1) * HD] for i in range(OWN)], axis=0)
    f_scores = [
        jnp.sum(q_own * f_s[n, 0][None], -1, keepdims=True) * scale for n in range(2)
    ]
    step_row = lax.broadcasted_iota(jnp.int32, (OWN, TOK, 1), 1)
    f_scores[1] = jnp.where(step_row >= REQS, f_scores[1], NEG)

    for cp in a_cp:
        cp.wait_recv()
    n_rows = OWN * TOK

    def to_row(v):
        return jnp.sum(jnp.where(lan == sub, v, 0.0), axis=0, keepdims=True)

    def to_col(v):
        return jnp.sum(jnp.where(lan == sub, v, 0.0), axis=1, keepdims=True)

    stat = jnp.concatenate(
        [a_recv[k, n_rows : n_rows + 16, :].astype(F32)[0:1] for k in range(N_P)], axis=0
    )
    totals = pltpu.roll(stat, 128 - n_rows, 1) + pltpu.roll(stat, 128 - 2 * n_rows, 1)
    f_scores = [to_row(f.reshape(n_rows, 1)) for f in f_scores]
    top = jnp.maximum(jnp.max(stat, axis=0, keepdims=True), jnp.maximum(f_scores[0], f_scores[1]))
    used = lan[0:1] < n_rows
    w_dev = jnp.exp(jnp.where(used, stat - top, NEG))
    w_new = [jnp.exp(jnp.where(used, f - top, NEG)) for f in f_scores]
    denom = jnp.sum(w_dev * totals, axis=0, keepdims=True) + w_new[0] + w_new[1]
    denom = 1.0 / jnp.where(used, denom, 1.0)
    w_dev = w_dev * denom
    numer = jnp.zeros((n_rows, HD), F32)
    for n in range(2):
        vals = jnp.broadcast_to(f_s[n, 1][None], (OWN, TOK, HD)).reshape(n_rows, HD)
        numer = numer + to_col(w_new[n] * denom) * vals
    for k in range(N_P):
        numer = numer + to_col(w_dev[k : k + 1]) * a_recv[k, 0:n_rows, :].astype(F32)
    attention = numer.reshape(OWN, TOK, HD)
    attention = jnp.concatenate([attention[i] for i in range(OWN)], axis=1).astype(BF16)

    for cp in rt_cp:
        cp.wait_recv()
    rt_cp = [send(rt.at[core, x], rt.at[core, x], at_x(k)) for k in range(1, NX)]

    def packed(v):
        half = v.shape[1] // 2
        return jnp.concatenate([v[:, 0:half], v[:, half:]], axis=0)

    def unpacked(v):
        return jnp.concatenate([v[0:TOK], v[TOK : 2 * TOK]], axis=1)

    res_cp.wait()
    at = pl.ds(pl.multiple_of(y * PAIR, PAIR), PAIR)
    for s in range(2):
        r_s[pl.ds(REQS * s, REQS), :] = res_v[s, :, at].astype(F32)
    ow_cp.wait()
    b_cp = []
    for k in (2, 1, 3, 0):
        yy = lax.rem(y + k, NY)
        term = jnp.dot(
            attention,
            ow_v[:, pl.ds(pl.multiple_of(yy * PAIR, PAIR), PAIR)],
            preferred_element_type=F32,
        )
        if k != 0:
            b_send[k] = packed(term).astype(BF16)
            b_cp.append(send(b_send.at[k], b_recv.at[k], at_y(k)))
    hidden = packed(jnp.where(zhi == 0, r_s[...], 0.0) + term)
    for k, cp in zip((2, 1, 3), b_cp):
        cp.wait_recv()
        hidden = hidden + b_recv[k].astype(F32)
    zr[0] = hidden.astype(BF16)

    z_cp = {k: send(zr.at[0], zr.at[k], at_z(k)) for k in Z_LABELS}
    for cp in rt_cp:
        cp.wait_recv()
    rt_cp = [send(rt.at[core], rt.at[core], sibling)]
    b_cp, a_cp = [], []

    def to_ring(hh, jb):
        piece = g_buf.at[hh, core, ia, jb]
        return [send(piece, piece, at_a(k)) for k in (2, 1, 3)]

    for hh in range(2):
        for n, o in enumerate(OFFSETS[hh]):
            if o != 0:
                z_cp[o].wait_recv()
            z_cp[(o + 4) % 8].wait_recv()
            hidden = zr[o].astype(F32) + zr[(o + 4) % 8].astype(F32)
            g_buf[hh, core, ia, ib, n] = hidden.astype(BF16)
        mine = g_buf.at[hh, core, ia, ib]
        b_cp.append({k: send(mine, mine, at_b(k)) for k in (2, 1, 3)})
    hid[0] = hidden[0:TOK]
    hid[1] = hidden[TOK : 2 * TOK]
    for hh in range(2):
        a_cp.append([to_ring(hh, ib)])
    gain_cp.wait()
    ssq[...] = jnp.zeros_like(ssq)
    for hh in range(2):
        for k in (1, 3, 2):
            b_cp[hh][k].wait_recv()
            a_cp[hh].append(to_ring(hh, lax.rem(ib + 4 - k, 4)))

    def prepare(hh, plane, jb):
        def step(ja, _):
            xx = (1 - plane) * ja + plane * jb
            yy = plane * ja + (1 - plane) * jb
            blocks = g_buf[hh, plane, ja, jb].astype(F32)
            rows = jnp.concatenate(
                [
                    blocks[:, 0:TOK].reshape(2 * TOK, PART),
                    blocks[:, TOK : 2 * TOK].reshape(2 * TOK, PART),
                ],
                axis=1,
            )
            sq = rows * rows
            while sq.shape[1] > 128:
                half = sq.shape[1] // 2
                sq = sq[:, 0:half] + sq[:, half:]
            at_row = pl.ds(
                pl.multiple_of((hh * 2 + plane) * (ALL // 4) + xx * (2 * TOK), 2 * TOK), 2 * TOK
            )
            at_col = pl.ds(pl.multiple_of(yy * PAIR, PAIR), PAIR)
            ssq[at_row, :] += sq
            rows_v[at_row, at_col] = (rows * gain_v[:, at_col]).astype(BF16)
            return 0

        for ja in range(4):
            step(ja, 0)

    from_core = [[], []]

    def absorb(hh, i):
        for cp in from_core[hh][i]:
            cp.wait_recv()
        prepare(hh, 1 - core, lax.rem(sib_ib + 4 - (0, 1, 3, 2)[i], 4))

    def receive(hh, first, last):
        order = (0, 1, 3, 2)

        def across(ja, jb):
            piece = g_buf.at[hh, core, ja, jb]
            return send(piece, piece, sibling)

        for i in range(first, last):
            jb = lax.rem(ib + 4 - order[i], 4)
            cps = [across(ia, jb)]
            for ka, cp in zip((2, 1, 3), a_cp[hh][i]):
                cp.wait_recv()
                cps.append(across(lax.rem(ia + 4 - ka, 4), jb))
            from_core[hh].append(cps)
            prepare(hh, core, jb)
            if i > 0:
                absorb(hh, i - 1)
        if last == 4:
            absorb(hh, 3)

    def experts(hh):
        here = slice(hh * (ALL // 2), (hh + 1) * (ALL // 2))
        spread = jnp.sum(ssq[here, :], -1, keepdims=True) * (1.0 / D)
        norm = lax.rsqrt(spread + 1e-06)
        coefs = rt[:, :, 2 * hh : 2 * hh + 2].reshape(ALL // 2, 128)
        lane = lax.broadcasted_iota(jnp.int32, (ALL // 2, 128), 1)
        all_up = jnp.dot(rows_v[here, :], wgu_v[...], preferred_element_type=F32)
        for j in range(2):
            coef = jnp.sum(jnp.where(lane == 2 * me + j, coefs, 0.0), -1, keepdims=True)
            both = all_up[:, 256 * j : 256 * j + 256]
            gate = both[:, 0:128] * norm
            up = both[:, 128:256] * norm
            inner = gate / (1.0 + jnp.exp(-gate)) * up
            act[here, 128 * j : 128 * j + 128] = (inner * coef).astype(BF16)

        def down_step(yy, _):
            at = pl.ds(pl.multiple_of(yy * PAIR, PAIR), PAIR)
            made = jnp.dot(act[here, :], wd_v[:, at], preferred_element_type=F32)
            made = made.reshape(2, NX * 2, TOK, PAIR)
            made = jnp.concatenate([made[..., 0:PART], made[..., PART:PAIR]], axis=2)
            made = made.astype(BF16).reshape(2, NX, 2, 2 * TOK, PART)
            p_buf[hh, 0, :, yy] = made[0]
            p_buf[hh, 1, yy] = made[1]
            return 0

        for k in range(NY):
            down_step(k, 0)

    order = (2, 1, 3, 0)

    def core_sends(hh):
        cps = []
        for kb in order:
            for ka in order:
                piece = (lax.rem(sib_ia + ka, 4), lax.rem(sib_ib + kb, 4))
                cps.append(send(p_buf.at[hh, 1 - core, *piece], s_buf.at[hh, *piece], sibling))
        return cps

    def ring_sends(hh, c_cp):
        cps = []
        for i, kb in enumerate(order):
            jb = lax.rem(ib + kb, 4)
            for n, ka in enumerate(order):
                ja = lax.rem(ia + ka, 4)
                c_cp[4 * i + n].wait_recv()
                both = p_buf[hh, core, ja, jb].astype(F32) + s_buf[hh, ja, jb].astype(F32)
                if ka != 0:
                    m_buf[hh, ja, jb] = both.astype(BF16)
                    cps.append(send(m_buf.at[hh, ja, jb], a_in.at[hh, i, ka], at_a(ka)))
                else:
                    n_buf[hh, i] = both
        return cps

    e_cp = []

    def last_sends(hh, ring_cp):
        for i, kb in enumerate(order):
            total = n_buf[hh, i]
            for n in range(3):
                ring_cp[3 * i + n].wait_recv()
                total = total + a_in[hh, i, order[n]].astype(F32)
            for n, o in enumerate(OFFSETS[hh]):
                t_buf[hh, i, n, 0] = total[n, 0:TOK]
                t_buf[hh, i, n, 1] = total[n, TOK : 2 * TOK]
                for kz in ((8 - o) % 8, 4 - o):
                    zz = lax.div(lax.rem(z + kz, N_Z), NZL)
                    if kb != 0 or kz != 0:
                        e_send[i, kz] = packed(t_buf[hh, i, n, zz]).astype(BF16)
                        cp = send(e_send.at[i, kz], e_recv.at[i, kz], at_bz(kb, kz))
                        e_cp.append((i, kz, cp))

    for cp in w_cp:
        cp.wait()
    for cp in wd_cp:
        cp.wait()
    receive(0, 0, 4)
    receive(1, 0, 1)
    for cp in rt_cp:
        cp.wait_recv()
    experts(0)
    c_0 = core_sends(0)
    receive(1, 1, 4)
    a_0 = ring_sends(0, c_0)
    experts(1)
    c_1 = core_sends(1)
    guest_cp.wait_recv()
    a_1 = ring_sends(1, c_1)
    last_sends(0, a_0)
    last_sends(1, a_1)
    n_last = len(sent) - len(e_cp)
    for cp in sent[:n_last]:
        cp.wait_send()
    result = packed(hid[zhi]) + packed(t_buf[1, 3, 1, zhi])
    for i, kz, cp in e_cp:
        cp.wait_recv()
        result = result + e_recv[i, kz].astype(F32)
    o_s[...] = unpacked(result)
    for s in range(2):
        out_ref[s] = o_s[REQS * s : REQS * (s + 1), :].astype(BF16)
    for cp in sent[n_last:]:
        cp.wait_send()


def shards(
    queries,
    fresh_entries,
    cache_blocks,
    lengths,
    migration,
    residual,
    out_weight,
    norm_gain,
    routes,
    route_gates,
    w_gate,
    w_up,
    w_down,
):
    vmem = pl.BlockSpec(memory_space=pltpu.VMEM)
    hbm = pl.BlockSpec(memory_space=pltpu.HBM)
    pair = (2 * TOK, PART)
    block = (2 * TOK, HALF)

    def buf(*shape, dtype=BF16):
        return pltpu.VMEM(shape, dtype)

    shapes = (
        jax.ShapeDtypeStruct((2, REQS, PART), BF16),
        jax.ShapeDtypeStruct((8, ROWS, 512), BF16),
    )
    return pl.pallas_call(
        kernel,
        out_shape=tuple(pltpu.VMEM(v.shape, v.dtype) for v in shapes),
        in_specs=[hbm] * 13,
        out_specs=(vmem, vmem),
        scratch_shapes=[
            buf(2, REQS, D),
            buf(2, REQS, 512),
            buf(1, REQS, dtype=jnp.int32),
            pltpu.SMEM((2, 8), jnp.int32),
            buf(2, REQS, D),
            buf(1, D, dtype=F32),
            buf(2, REQS, TOPK, dtype=jnp.int32),
            buf(2, REQS, TOPK, dtype=F32),
            buf(REQS, BLOCKS, ROWS, 512),
            buf(PART, D),
            buf(D, 512),
            buf(256, D),
            buf(8, ROWS, 512),
            buf(TOK, D, dtype=F32),
            buf(QH * TOK, HD),
            buf(2, 2, TOK, HD, dtype=F32),
            buf(TOK, PAIR, dtype=F32),
            buf(N_P, OWN * TOK + 16, HD),
            buf(N_P, OWN * TOK + 16, HD),
            buf(NY, *pair),
            buf(NY, *pair),
            buf(N_Z, *pair),
            buf(2, TOK, PART, dtype=F32),
            buf(2, NX, NZL, TOK, 128, dtype=F32),
            buf(2, 2, 4, 4, 2, *pair),
            buf(ALL, D),
            buf(ALL, 128, dtype=F32),
            buf(ALL, 256),
            buf(2, 2, 4, 4, 2, *pair),
            buf(2, 4, 4, 2, *pair),
            buf(2, 4, 4, 2, *pair),
            buf(2, 4, 4, 2, *pair),
            buf(2, 4, 2, *pair, dtype=F32),
            buf(2, 4, 2, 2, TOK, PART, dtype=F32),
            buf(4, N_Z, *block),
            buf(4, N_Z, *block),
            buf(TOK, PART, dtype=F32),
            pltpu.SemaphoreType.DMA((24,)),
            pltpu.SemaphoreType.DMA((N_SEMS,)),
            pltpu.SemaphoreType.DMA((N_SEMS,)),
        ],
        compiler_params=pltpu.CompilerParams(
            collective_id=0, has_side_effects=True, vmem_limit_bytes=60 * MIB
        ),
        cost_estimate=pl.CostEstimate(
            flops=2_000_000_000, bytes_accessed=13 * MIB, transcendentals=200_000
        ),
    )(
        queries,
        fresh_entries,
        cache_blocks,
        lengths.reshape(1, REQS),
        migration.T,
        residual,
        out_weight,
        norm_gain.reshape(1, D),
        routes,
        route_gates,
        w_gate,
        w_up,
        w_down,
    )


def solution(mesh):
    in_specs = (
        P(None, "dp", None),
        P(None, "dp", None),
        P("dp", None, "expert", None),
        P("dp"),
        P("dp", None),
        P(None, "dp", None),
        P("expert", None),
        P(),
        P(None, "dp", None),
        P(None, "dp", None),
        P("dp", None, "expert"),
        P("dp", None, "expert"),
        P("dp", "expert", None),
    )
    out_specs = (P(None, "dp", "expert"), P("dp", "expert", None))
    return jax.shard_map(shards, mesh=mesh, in_specs=in_specs, out_specs=out_specs, check_vma=False)
```
